32 devices in a mesh: gx: 4 (over z), gy: 8 (over y, x, core).
Axes of the slice: x: 2, y: 2, z: 4, core: 2. Of those that a mesh axis runs over, the one named last changes fastest.
Arguments:
- leaf_front: float32 [6144, 12288], P('gx', 'gy'), may hold values from -18 to 18, as said below
- place_pairs: int32 [4, 64], P('gx', 'gy'), may hold values from 0 to 11, as said below
- place_quads: int32 [4, 64], P('gx', 'gy'), may hold values from 0 to 11, as said below
Outputs:
- pair_panel: float32 [6144, 4096], P('gx', 'gy')
- quad_panel: float32 [6144, 4096], P('gx', 'gy')
- quad_update: float32 [4096, 8192], P('gx', 'gy')
The draws below stay inside these ranges and needn't reach their ends.
Inputs may be any that keep to these rules, and one draw needn't show every extreme that they name: `leaf_front`: each tile is symmetric positive definite. `place_pairs`: each device's 8 entries are distinct; the two devices (q, j) and (q + 2, j) both name blocks 0 to 3, and each names 4 of the other blocks that the other does not name. `place_quads`: devices (q, j) and (q + 2, j) hold equal rows; each row's 8 entries are distinct; the rows of (q, r) and (q, r + 4) both name blocks 0 to 3, and each names 4 of the other blocks that the other does not name.
All inputs are finite; a program needn't handle non-finite values.
Results may differ from the reference program's by a relative error of at most 0.0003.
Values sent between devices are 32-bit elements; how exact they have to be, the bound alone decides.
No kernel may reach another device: no remote copies, remote signals or barrier semaphores. Data moves between devices by JAX's collectives and lax.ppermute only.
A program may use at most 192 MiB of HBM per device.

```python
import jax
import jax.numpy as jnp
from jax import lax

BLK = 128
KB = 8
NI = 512
KS = 4
NB = 1024
NS = 512
NJ = 1536
NL = 1536
N_GX = 4
N_GY = 8


def draw_leaf_front(key, part):
    devices_total = N_GX * N_GY
    subkeys = jax.random.split(jax.random.fold_in(key, 3), devices_total)
    gen_rank = max(NL // 4, 8)

    def one_device(device_key):
        key_gen, key_diag = jax.random.split(device_key, 2)
        generator = jnp.clip(jax.random.normal(key_gen, (NL, gen_rank), jnp.float32), -4.0, 4.0)
        diag_shift = jnp.exp(jax.random.uniform(key_diag, (NL,), jnp.float32, -0.6931, 0.4055))
        gram_matrix = jnp.dot(generator, generator.T, precision=lax.Precision.HIGHEST) / gen_rank
        gram_matrix = 0.5 * (gram_matrix + gram_matrix.T)
        matrix = gram_matrix + jnp.diag(diag_shift)
        return matrix
    matrices = jax.vmap(one_device)(subkeys)
    return matrices.reshape(N_GX, N_GY, NL, NL).transpose(0, 2, 1, 3).reshape(N_GX * NL, N_GY * NL)


def placement_rows(key, parity):
    subkeys = jax.random.split(key, parity.shape[0])

    def one_row(row_key, side):
        targets = jnp.concatenate([jnp.arange(KS, dtype=jnp.int32), (KS + side * (KB - KS) + jnp.arange(KB - KS)).astype(jnp.int32)])
        return jax.random.permutation(row_key, targets)
    return jax.vmap(one_row)(subkeys, parity)


def draw_place_pairs(key, part):
    devices_total = N_GX * N_GY
    parity = (jnp.arange(devices_total) // N_GY >= N_GX // 2).astype(jnp.int32)
    indices = placement_rows(jax.random.fold_in(key, 11), parity)
    return indices.reshape(N_GX, N_GY * KB)


def draw_place_quads(key, part):
    groups_total = N_GX // 2 * N_GY
    parity = (jnp.arange(groups_total) % N_GY >= N_GY // 2).astype(jnp.int32)
    indices = placement_rows(jax.random.fold_in(key, 23), parity).reshape(N_GX // 2, N_GY, KB)
    return jnp.concatenate([indices, indices], axis=0).reshape(N_GX, N_GY * KB)


def setup_inputs(seed: int = 0) -> dict:
    seeds = jax.random.split(jax.random.key(seed), 4)
    return {
        "leaf_front": draw_leaf_front(jax.random.fold_in(seeds[3], 71), 0),
        "place_pairs": draw_place_pairs(jax.random.fold_in(seeds[3], 71), 0),
        "place_quads": draw_place_quads(jax.random.fold_in(seeds[3], 71), 0),
    }


def leaf_update(front_tile):
    interior = jnp.linalg.cholesky(front_tile[:NI, :NI])
    coupled = jax.scipy.linalg.solve_triangular(interior, front_tile[:NI, NI:], lower=True)
    return front_tile[NI:, NI:] - jnp.dot(coupled.T, coupled, precision=lax.Precision.HIGHEST)

def extend_add(update, placement):
    indices = (placement[:, None] * BLK + jnp.arange(BLK)[None, :]).reshape(-1).astype(jnp.int32)
    return jnp.zeros((NJ, NJ), update.dtype).at[indices[:, None], indices[None, :]].add(update)

def partial_factor(joined):
    corner = jnp.linalg.cholesky(joined[:NS, :NS])
    coupled = jax.scipy.linalg.solve_triangular(corner, joined[:NS, NS:], lower=True)
    factor_panel = jnp.concatenate([corner, coupled.T], axis=0)
    update = joined[NS:, NS:] - jnp.dot(coupled.T, coupled, precision=lax.Precision.HIGHEST)
    return (factor_panel, update)

def merge_children(operands):
    first_update, first_place, second_update, second_place = operands
    joined = extend_add(first_update, first_place) + extend_add(second_update, second_place)
    return partial_factor(joined)

def tiles_out(stacked, rows_rep, cols_rep):
    spread = jnp.tile(stacked, (rows_rep, cols_rep, 1, 1))
    return spread.transpose(0, 2, 1, 3).reshape(spread.shape[0] * spread.shape[2], spread.shape[1] * spread.shape[3])

def reference(leaf_front, place_pairs, place_quads):
    all_fronts = leaf_front.reshape(N_GX, NL, N_GY, NL).transpose(0, 2, 1, 3).reshape(N_GX * N_GY, NL, NL)
    leaf_updates = lax.map(leaf_update, all_fronts).reshape(N_GX, N_GY, NB, NB)
    pair_places = place_pairs.reshape(N_GX, N_GY, KB)
    quad_places = place_quads.reshape(N_GX, N_GY, KB)
    half_gx = N_GX // 2
    half_gy = N_GY // 2
    level_one = (leaf_updates[:half_gx].reshape(-1, NB, NB), pair_places[:half_gx].reshape(-1, KB), leaf_updates[half_gx:].reshape(-1, NB, NB), pair_places[half_gx:].reshape(-1, KB))
    panels_one, updates_one = lax.map(merge_children, level_one)
    panels_one = panels_one.reshape(half_gx, N_GY, NJ, NS)
    updates_one = updates_one.reshape(half_gx, N_GY, NB, NB)
    level_two = (updates_one[:, :half_gy].reshape(-1, NB, NB), quad_places[:half_gx, :half_gy].reshape(-1, KB), updates_one[:, half_gy:].reshape(-1, NB, NB), quad_places[:half_gx, half_gy:].reshape(-1, KB))
    panels_two, updates_two = lax.map(merge_children, level_two)
    panels_two = panels_two.reshape(half_gx, half_gy, NJ, NS)
    updates_two = updates_two.reshape(half_gx, half_gy, NB, NB)
    return (tiles_out(panels_one, 2, 1), tiles_out(panels_two, 2, 2), tiles_out(updates_two, 2, 2))
```

```python
import jax
import jax.numpy as jnp
from jax import lax
from jax.experimental import pallas as pl
from jax.experimental.pallas import tpu as pltpu
from jax.sharding import PartitionSpec as P

f32 = jnp.float32
bf16 = jnp.bfloat16
NT = (((1,), (1,)), ((), ()))
TN = (((0,), (0,)), ((), ()))
BLK = 128
KB = 8
KS = 4
NS = KS * BLK
NB = KB * BLK
LOWER = [(a, b) for a in range(KS) for b in range(a + 1)]
VMEM = pl.BlockSpec(memory_space=pltpu.VMEM)
SMEM = pl.BlockSpec(memory_space=pltpu.SMEM)
ANY = pl.BlockSpec(memory_space=pl.ANY)


def sds(*shape):
    return jax.ShapeDtypeStruct(shape, f32)


def call(body, out, ins, outs, scratch, us, args, alias=None):
    cost = pl.CostEstimate(flops=int(us * 1e9), bytes_accessed=int(us * 3.5e6), transcendentals=0)
    return pl.pallas_call(
        body,
        out_shape=out,
        in_specs=ins,
        out_specs=outs,
        scratch_shapes=scratch,
        cost_estimate=cost,
        input_output_aliases=alias or {},
        compiler_params=pltpu.CompilerParams(vmem_limit_bytes=48 * 1024 * 1024),
    )(*args)


def split(x):
    hi = x.astype(bf16)
    return hi, (x - hi.astype(f32)).astype(bf16)


def dot(a, b, dims):
    return lax.dot_general(a, b, dims, preferred_element_type=f32)


def mm3(a, b, dims):
    return dot(a[0], b[0], dims) + (dot(a[0], b[1], dims) + dot(a[1], b[0], dims))


def row(x, k):
    return jnp.broadcast_to(x[k : k + 1, :], x.shape)


def col(x, j):
    return jnp.broadcast_to(x[:, j : j + 1], (8, BLK))


def factor_block(block):
    ri = lax.broadcasted_iota(jnp.int32, (8, BLK), 0)
    ci = lax.broadcasted_iota(jnp.int32, (8, BLK), 1)
    count = BLK // 8
    left = [block[8 * t : 8 * t + 8, :] for t in range(count)]
    right = [jnp.where(ci == ri + 8 * t, 1.0, 0.0).astype(f32) for t in range(count)]
    upper, inverse = [], []
    for s in range(count):
        here = [col(left[s], 8 * s + k) for k in range(8)]
        ahead = [col(left[s + 1], 8 * s + k) for k in range(8)] if s + 1 < count else None
        a, t = left[s], right[s]
        pivots = None
        for k in range(8):
            pivot = row(here[k], k)
            inv = pl.reciprocal(pivot, approx=True)
            inv = inv * (2.0 - pivot * inv)
            pivots = pivot if k == 0 else jnp.where(ri == k, pivot, pivots)
            mult = jnp.where(ri > k, here[k], 0.0) * inv
            rows = {m: row(here[m], k) for m in range(k + 1, 8)}
            row_a, row_t = row(a, k), row(t, k)
            for m in range(k + 1, 8):
                here[m] = here[m] - mult * rows[m]
            a = a - mult * row_a
            t = t - mult * row_t
            if ahead is not None:
                mult = ahead[k] * inv
                for m in range(k + 1, 8):
                    ahead[m] = ahead[m] - mult * rows[m]
                left[s + 1] = left[s + 1] - mult * row_a
                right[s + 1] = right[s + 1] - mult * row_t
        scale = lax.rsqrt(pivots)
        a = jnp.where(ci >= ri + 8 * s, a * scale, 0.0)
        t = t * scale
        upper.append(a)
        inverse.append(t)
        if s + 2 < count:
            ah = a.astype(bf16).astype(f32)
            th = t.astype(bf16).astype(f32)
            al, tl, zero = a - ah, t - th, jnp.zeros_like(a)
            lhs = jnp.concatenate([ah, ah, al, zero], 0).astype(bf16)
            rhs_a = jnp.concatenate([ah, al, ah, zero], 0)
            rhs_t = jnp.concatenate([th, tl, th, zero], 0)
            rhs = jnp.concatenate([rhs_a, rhs_t], 1).astype(bf16)
            outer = dot(lhs, rhs, TN)
            for q in range(s + 2, count):
                left[q] = left[q] - outer[8 * q : 8 * q + 8, :BLK]
                right[q] = right[q] - outer[8 * q : 8 * q + 8, BLK:]
    return jnp.concatenate(upper, 0), jnp.concatenate(inverse, 0)


def factor(work, lower, inv):
    for k in range(KS):
        o, e = BLK * k, BLK * (k + 1)
        upper, inverse = factor_block(work[o:e, o:e])
        inv[k] = inverse
        lower[o:e, o:e] = upper.T
        if k + 1 < KS:
            lower[o:e, e:] = jnp.zeros((BLK, NS - e), f32)
            below = mm3(split(work[e:, o:e]), split(inverse), NT)
            lower[e:, o:e] = below
            pair = split(below)
            work[e:, e:] = work[e:, e:] - mm3(pair, pair, NT)


def solve(x, lower, inv):
    for k in range(KS):
        o, e = BLK * k, BLK * (k + 1)
        done = mm3(split(x[:, o:e]), split(inv[k]), NT)
        x[:, o:e] = done
        if k + 1 < KS:
            x[:, e:] = x[:, e:] - mm3(split(done), split(lower[e:, o:e]), NT)


def ranks(values):
    out = []
    for a, va in enumerate(values):
        r = jnp.int32(0)
        for b, vb in enumerate(values):
            if a != b:
                r = r + (vb < va).astype(jnp.int32)
        out.append(r)
    return out


def sort_blocks(place, order):
    values = [place[0, a] for a in range(KB)]
    for a, r in enumerate(ranks(values)):
        order[r] = jnp.int32(a)


def at(start):
    return pl.ds(pl.multiple_of(start, BLK), BLK)


def leaf_a(front, place, corner, w_out, a, lower, inv, ss, order, sems):
    sort_blocks(place, order)
    copies = [pltpu.make_async_copy(front.at[0:NS, 0:NS], a, sems.at[0])]
    copies[0].start()
    for t in range(KB):
        c = pltpu.make_async_copy(
            front.at[at(NS + BLK * order[t]), 0:NS], w_out.at[BLK * t : BLK * t + BLK, :], sems.at[1 + t]
        )
        c.start()
        copies.append(c)
    for n, (i, j) in enumerate(LOWER):
        c = pltpu.make_async_copy(
            front.at[at(NS + BLK * order[i]), at(NS + BLK * order[j])], ss.at[n], sems.at[1 + KB + n]
        )
        c.start()
        copies.append(c)
    copies[0].wait()
    factor(a, lower, inv)
    for c in copies[1:]:
        c.wait()
    solve(w_out, lower, inv)
    w = split(w_out[0:NS, :])
    for i in range(KS):
        rows = slice(BLK * i, BLK * i + BLK)
        left = tuple(v[rows] for v in w)
        right = tuple(v[: BLK * i + BLK] for v in w)
        gram = mm3(left, right, NT)
        for j in range(i + 1):
            n = LOWER.index((i, j))
            corner[n] = ss[n] - gram[:, BLK * j : BLK * j + BLK]


def leaf_b(front, place, w, rs, rr, rr_low, f_rs, f_rr, order, sems):
    sort_blocks(place, order)
    copies = []
    for i in range(KS):
        for j in range(KB):
            dst = f_rs if j < KS else f_rr
            c = pltpu.make_async_copy(
                front.at[at(NS + BLK * order[KS + i]), at(NS + BLK * order[j])],
                dst.at[BLK * i : BLK * i + BLK, BLK * (j % KS) : BLK * (j % KS) + BLK],
                sems.at[i * KB + j],
            )
            c.start()
            copies.append(c)
    ws, wr = split(w[0:NS, :]), split(w[NS:, :])
    g_rs = mm3(wr, ws, NT)
    g_rr = mm3(wr, wr, NT)
    for c in copies:
        c.wait()
    rs[...] = f_rs[...] - g_rs
    rr[...] = f_rr[...] - g_rr
    for n, (i, j) in enumerate(LOWER):
        rr_low[n] = rr[BLK * i : BLK * i + BLK, BLK * j : BLK * j + BLK]


def merge_a(mine, other, rs, lower, inv, v, work):
    for n, (i, j) in enumerate(LOWER):
        block = mine[n] + other[n]
        work[BLK * i : BLK * i + BLK, BLK * j : BLK * j + BLK] = block
        if i != j:
            work[BLK * j : BLK * j + BLK, BLK * i : BLK * i + BLK] = block.T
    v[...] = rs[...]
    factor(work, lower, inv)
    solve(v, lower, inv)


def joined_places(place, place_other, order):
    sort_blocks(place, order)
    mine = [place[0, order[KS + i]] for i in range(KS)]
    sort_blocks(place_other, order)
    return mine + [place_other[0, order[KS + i]] for i in range(KS)]


def next_ranks(places, place_next):
    return ranks([place_next[0, p - KS] for p in places])


def write_panel(panel, lower, v, places):
    panel[0:NS, :] = lower[...]
    for e in range(KB):
        panel[at(BLK * places[e]), :] = v[BLK * e : BLK * e + BLK, :]


def merge_b(lower, inv, v_mine, rs_other, rr, place, place_other, place_next, panel, update, v, vs, order):
    v[0:NS, :] = v_mine[...]
    v[NS:, :] = rs_other[...]
    solve(v.at[NS:, :], lower, inv)
    places = joined_places(place, place_other, order)
    write_panel(panel, lower, v, places)
    spots = next_ranks(places, place_next)
    for e in range(KB):
        vs[at(BLK * spots[e]), :] = v[BLK * e : BLK * e + BLK, :]
    pair = split(vs[...])
    for t in range(KB):
        rows = slice(BLK * t, BLK * t + BLK)
        cols = slice(0, BLK * t + BLK)
        update[rows, cols] = -mm3(tuple(p[rows] for p in pair), tuple(p[cols] for p in pair), NT)
    for e in range(KS):
        for f in range(KS):
            r, c = at(BLK * spots[e]), at(BLK * spots[f])
            update[r, c] = update[r, c] + rr[BLK * e : BLK * e + BLK, BLK * f : BLK * f + BLK]


def other_blocks(rr_other):
    blocks = {}
    for n, (i, j) in enumerate(LOWER):
        blocks[i, j] = rr_other[n]
        if i != j:
            blocks[j, i] = rr_other[n].T
    return blocks


def add_other(update, rr_other, spots, want):
    for (e, f), block in other_blocks(rr_other).items():
        se, sf = spots[KS + e], spots[KS + f]

        @pl.when(want(se, sf))
        def _():
            r, c = at(BLK * se), at(BLK * sf)
            update[r, c] = update[r, c] + block


def next_corner(update, rr_other, place, place_other, place_next, corner, work, order, sem):
    copy = pltpu.make_async_copy(update.at[0:NS, 0:NS], work, sem)
    copy.start()
    spots = next_ranks(joined_places(place, place_other, order), place_next)
    copy.wait()
    add_other(work, rr_other, spots, lambda a, b: (a < KS) & (b <= a))
    for n, (i, j) in enumerate(LOWER):
        corner[n] = work[BLK * i : BLK * i + BLK, BLK * j : BLK * j + BLK]


def next_rest(update, rr_other, place, place_other, place_next, rs, rr, rr_low, work, order, sem):
    copy = pltpu.make_async_copy(update.at[NS:NB, :], work.at[NS:NB, :], sem)
    copy.start()
    spots = next_ranks(joined_places(place, place_other, order), place_next)
    copy.wait()
    add_other(work, rr_other, spots, lambda a, b: (a >= KS) & (b <= a))
    rs[...] = work[NS:, 0:NS]
    for n, (i, j) in enumerate(LOWER):
        block = work[NS + BLK * i : NS + BLK * i + BLK, NS + BLK * j : NS + BLK * j + BLK]
        rr_low[n] = block
        rr[BLK * i : BLK * i + BLK, BLK * j : BLK * j + BLK] = block
        if i != j:
            rr[BLK * j : BLK * j + BLK, BLK * i : BLK * i + BLK] = block.T


def last_b(lower, inv, v_mine, rs_other, rr, place, place_other, panel, update, v, vs, order):
    v[0:NS, :] = v_mine[...]
    v[NS:, :] = rs_other[...]
    solve(v.at[NS:, :], lower, inv)
    places = joined_places(place, place_other, order)
    write_panel(panel, lower, v, places)
    vs[...] = panel[NS:, :]
    pair = split(vs[...])
    for t in range(KB):
        rows = slice(BLK * t, BLK * t + BLK)
        update[rows, :] = -mm3(tuple(p[rows] for p in pair), pair, NT)
    for e in range(KS):
        for f in range(KS):
            r, c = at(BLK * (places[e] - KS)), at(BLK * (places[f] - KS))
            update[r, c] = update[r, c] + rr[BLK * e : BLK * e + BLK, BLK * f : BLK * f + BLK]


def last_add(update_in, rr_other, place, place_other, update, order, buf, sems_in, sems_out):
    del update_in
    places = joined_places(place, place_other, order)
    blocks = other_blocks(rr_other)
    ins, outs = [], []
    for n, (e, f) in enumerate(blocks):
        r, c = at(BLK * (places[KS + e] - KS)), at(BLK * (places[KS + f] - KS))
        ins.append(pltpu.make_async_copy(update.at[r, c], buf.at[n], sems_in.at[n]))
        outs.append(pltpu.make_async_copy(buf.at[n], update.at[r, c], sems_out.at[n]))
        ins[-1].start()
    for n, key in enumerate(blocks):
        ins[n].wait()
        buf[n] = buf[n] + blocks[key]
        outs[n].start()
    for c in outs:
        c.wait()


def shards(leaf_front, place_pairs, place_quads):
    dma = pltpu.SemaphoreType.DMA
    tri = len(LOWER)
    half_cols = lax.axis_size("gx") // 2
    half_rows = lax.axis_size("gy") // 2

    def partner(x, axis, half):
        return lax.ppermute(x, axis, [(i, (i + half) % (2 * half)) for i in range(2 * half)])

    pairs_other = partner(place_pairs, "gx", half_cols)
    quads_other = partner(place_quads, "gy", half_rows)
    order = pltpu.SMEM((KB,), jnp.int32)

    corner, w = call(
        leaf_a, (sds(tri, BLK, BLK), sds(NB, NS)), [ANY, SMEM], [VMEM, VMEM],
        [pltpu.VMEM((NS, NS), f32), pltpu.VMEM((NS, NS), f32), pltpu.VMEM((KS, BLK, BLK), f32),
         pltpu.VMEM((tri, BLK, BLK), f32), order, dma((1 + KB + tri,))],
        25, (leaf_front, place_pairs))
    corner_other = partner(corner, "gx", half_cols)
    rs, rr, rr_low = call(
        leaf_b, (sds(NS, NS), sds(NS, NS), sds(tri, BLK, BLK)), [ANY, SMEM, VMEM], [VMEM] * 3,
        [pltpu.VMEM((NS, NS), f32), pltpu.VMEM((NS, NS), f32), order, dma((KS * KB,))],
        5, (leaf_front, place_pairs, w))
    rs_other = partner(rs, "gx", half_cols)
    rr_other = partner(rr_low, "gx", half_cols)

    shapes_a = (sds(NS, NS), sds(KS, BLK, BLK), sds(NS, NS))
    lower, inv, v = call(
        merge_a, shapes_a, [VMEM] * 3, [VMEM] * 3, [pltpu.VMEM((NS, NS), f32)], 25, (corner, corner_other, rs))
    scratch_b = [pltpu.VMEM((NB, NS), f32), pltpu.VMEM((NB, NS), f32), order]
    pair_panel, update = call(
        merge_b, (sds(NS + NB, NS), sds(NB, NB)), [VMEM] * 5 + [SMEM] * 3, [VMEM] * 2, scratch_b,
        10, (lower, inv, v, rs_other, rr, place_pairs, pairs_other, place_quads))
    rest = (update, rr_other, place_pairs, pairs_other, place_quads)
    specs = [ANY, VMEM] + [SMEM] * 3
    corner = call(
        next_corner, sds(tri, BLK, BLK), specs, VMEM,
        [pltpu.VMEM((NS, NS), f32), order, dma], 2, rest)
    corner_other = partner(corner, "gy", half_rows)
    rs, rr, rr_low = call(
        next_rest, (sds(NS, NS), sds(NS, NS), sds(tri, BLK, BLK)), specs, [VMEM] * 3,
        [pltpu.VMEM((NB, NB), f32), order, dma], 3, rest)
    rs_other = partner(rs, "gy", half_rows)
    rr_other = partner(rr_low, "gy", half_rows)

    lower, inv, v = call(
        merge_a, shapes_a, [VMEM] * 3, [VMEM] * 3, [pltpu.VMEM((NS, NS), f32)], 25, (corner, corner_other, rs))
    quad_panel, quad_update = call(
        last_b, (sds(NS + NB, NS), sds(NB, NB)), [VMEM] * 5 + [SMEM] * 2, [VMEM] * 2, scratch_b,
        12, (lower, inv, v, rs_other, rr, place_quads, quads_other))
    pairs = KS * KS
    quad_update = call(
        last_add, sds(NB, NB), [ANY, VMEM] + [SMEM] * 2, ANY,
        [order, pltpu.VMEM((pairs, BLK, BLK), f32), dma((pairs,)), dma((pairs,))],
        2, (quad_update, rr_other, place_quads, quads_other), {0: 0})
    return pair_panel, quad_panel, quad_update


def solution(mesh):
    spec = P("gx", "gy")
    return jax.shard_map(
        shards, mesh=mesh, in_specs=(spec, spec, spec), out_specs=(spec, spec, spec), check_vma=False
    )
```

```python
import jax
import jax.numpy as jnp
from jax import lax
from jax.experimental import pallas as pl
from jax.experimental.pallas import tpu as pltpu
from jax.sharding import PartitionSpec as P

f32 = jnp.float32
bf16 = jnp.bfloat16
NT = (((1,), (1,)), ((), ()))
TN = (((0,), (0,)), ((), ()))
BLK = 128
KB = 8
KS = 4
NS = KS * BLK
NB = KB * BLK
NJ = NS + NB
LOWER = [(a, b) for a in range(KS) for b in range(a + 1)]
VMEM = pl.BlockSpec(memory_space=pltpu.VMEM)
SMEM = pl.BlockSpec(memory_space=pltpu.SMEM)
HBM = pl.BlockSpec(memory_space=pltpu.HBM)


def sds(*shape):
    return jax.ShapeDtypeStruct(shape, f32)


def call(body, out, ins, outs, scratch, args, vmem=32):
    return pl.pallas_call(
        body,
        out_shape=out,
        in_specs=ins,
        out_specs=outs,
        scratch_shapes=scratch,
        cost_estimate=pl.CostEstimate(flops=1000, bytes_accessed=1000, transcendentals=0),
        compiler_params=pltpu.CompilerParams(vmem_limit_bytes=vmem * 1024 * 1024),
    )(*args)


def split(x):
    hi = x.astype(bf16)
    return hi, (x - hi.astype(f32)).astype(bf16)


def dot(a, b, dims):
    return lax.dot_general(a, b, dims, preferred_element_type=f32)


def mm3(a, b):
    return dot(jnp.concatenate([a[0], a[0], a[1]], 1), jnp.concatenate([b[0], b[1], b[0]], 1), NT)


def row(x, k):
    return jnp.broadcast_to(x[k : k + 1, :], x.shape)


def col(x, j):
    return jnp.broadcast_to(x[:, j : j + 1], (8, BLK))


def factor_block(block):
    ri = lax.broadcasted_iota(jnp.int32, (8, BLK), 0)
    ci = lax.broadcasted_iota(jnp.int32, (8, BLK), 1)
    count, wide = BLK // 8, 4
    left = [block[8 * t : 8 * t + 8, :] for t in range(count)]
    right = [jnp.where(ci == ri + 8 * t, 1.0, 0.0).astype(f32) for t in range(count)]
    upper, inverse = [], []
    here = [col(left[0], k) for k in range(8)]
    for s in range(count):
        end = (s // wide + 1) * wide
        ahead = {w: [col(left[w], 8 * s + k) for k in range(8)] for w in range(s + 1, min(end + 1, count))}
        following = [col(left[s + 1], 8 * s + 8 + k) for k in range(8)] if s + 1 < count else None
        a, t = left[s], right[s]
        pivots = None
        for k in range(8):
            pivot = row(here[k], k)
            inv = pl.reciprocal(pivot, approx=True)
            pivots = pivot if k == 0 else jnp.where(ri == k, pivot, pivots)
            mult = jnp.where(ri > k, here[k], 0.0) * inv
            rows = {m: row(here[m], k) for m in range(k + 1, 8)}
            row_a, row_t = row(a, k), row(t, k)
            for m in range(k + 1, 8):
                here[m] = here[m] - mult * rows[m]
            a = a - mult * row_a
            t = t - mult * row_t
            for w, cols in ahead.items():
                mult = cols[k] * inv
                if w == s + 1:
                    following = [f - mult * row(cols[k], m) for m, f in enumerate(following)]
                for m in range(k + 1, 8):
                    cols[m] = cols[m] - mult * rows[m]
                left[w] = left[w] - mult * row_a
                right[w] = right[w] - mult * row_t
        here = following
        scale = lax.rsqrt(pivots)
        upper.append(a * scale)
        inverse.append(t * scale)
        if s + 1 == end and end + 1 < count:
            ah, al = split(jnp.concatenate(upper[-wide:], 0))
            th, tl = split(jnp.concatenate(inverse[-wide:], 0))
            lhs = jnp.concatenate([ah, ah, al], 0)
            rhs_a = jnp.concatenate([ah, al, ah], 0)
            rhs_t = jnp.concatenate([th, tl, th], 0)
            outer = dot(lhs, jnp.concatenate([rhs_a, rhs_t], 1), TN)
            for q in range(end + 1, count):
                left[q] = left[q] - outer[8 * q : 8 * q + 8, :BLK]
                right[q] = right[q] - outer[8 * q : 8 * q + 8, BLK:]
    return jnp.concatenate(inverse, 0)


def factor(work, x, lower, inv, corner):
    ri = lax.broadcasted_iota(jnp.int32, (NS, BLK), 0)
    ci = lax.broadcasted_iota(jnp.int32, (NS, BLK), 1)

    def finish(k, inverse):
        here = at(BLK * k)
        inv[k] = inverse
        lower[:, here] = jnp.where(ri >= ci + BLK * k, mm3(split(work[:, here]), split(inverse)), 0.0)
        if not isinstance(k, int) or k + 1 < KS:
            then = at(BLK * jnp.minimum(k + 1, KS - 1))
            pair = split(lower[then, here])
            corner[...] = work[then, then] - mm3(pair, pair)

    def update(k):
        here = at(BLK * k)
        pair = split(lower[:, here])
        work[...] = work[...] - mm3(pair, pair)
        done = mm3(split(x[:, here]), split(inv[k]))
        x[...] = x[...] - mm3(split(done), pair)
        x[:, here] = done

    def step(k, carry):
        inverse = factor_block(corner[...])
        update(k - 1)
        finish(k, inverse)
        return carry

    finish(0, factor_block(work[0:BLK, 0:BLK]))
    lax.fori_loop(1, KS, step, 0)
    x[:, NS - BLK :] = mm3(split(x[:, NS - BLK :]), split(inv[KS - 1]))


def solve(x, lower, inv):
    for k in range(KS):
        o, e = BLK * k, BLK * (k + 1)
        done = mm3(split(x[:, o:e]), split(inv[k]))
        x[:, o:e] = done
        if k + 1 < KS:
            x[:, e:] = x[:, e:] - mm3(split(done), split(lower[e:, o:e]))


def ranks(values):
    out = []
    for a, va in enumerate(values):
        r = jnp.int32(0)
        for b, vb in enumerate(values):
            if a != b:
                r = r + (vb < va).astype(jnp.int32)
        out.append(r)
    return out


def sort_blocks(place, order):
    values = [place[0, a] for a in range(KB)]
    for a, r in enumerate(ranks(values)):
        order[r] = jnp.int32(a)


def at(start):
    return pl.ds(pl.multiple_of(start, BLK), BLK)


def leaf_a(front, place, corner, w_out, a, lower, inv, next_block, ss, order, sems):
    sort_blocks(place, order)
    copies = [pltpu.make_async_copy(front.at[0:NS, 0:NS], a, sems.at[0])]
    copies[0].start()
    for t in range(KB):
        c = pltpu.make_async_copy(
            front.at[at(NS + BLK * order[t]), 0:NS], w_out.at[BLK * t : BLK * t + BLK, :], sems.at[1 + t]
        )
        c.start()
        copies.append(c)
    for n, (i, j) in enumerate(LOWER):
        c = pltpu.make_async_copy(
            front.at[at(NS + BLK * order[i]), at(NS + BLK * order[j])], ss.at[n], sems.at[1 + KB + n]
        )
        c.start()
        copies.append(c)
    for c in copies:
        c.wait()
    factor(a, w_out, lower, inv, next_block)
    w = split(w_out[0:NS, :])
    for i in range(KS):
        rows = slice(BLK * i, BLK * i + BLK)
        left = tuple(v[rows] for v in w)
        right = tuple(v[: BLK * i + BLK] for v in w)
        gram = mm3(left, right)
        for j in range(i + 1):
            n = LOWER.index((i, j))
            corner[n] = ss[n] - gram[:, BLK * j : BLK * j + BLK]


def leaf_b(front, place, w, rs, rs_a, rs_b, rr_low, f_rs, f_rr, order, sems):
    sort_blocks(place, order)
    copies = []
    for i in range(KS):
        for j in range(KB):
            dst = f_rs if j < KS else f_rr
            c = pltpu.make_async_copy(
                front.at[at(NS + BLK * order[KS + i]), at(NS + BLK * order[j])],
                dst.at[BLK * i : BLK * i + BLK, BLK * (j % KS) : BLK * (j % KS) + BLK],
                sems.at[i * KB + j],
            )
            c.start()
            copies.append(c)
    ws, wr = split(w[0:NS, :]), split(w[NS:, :])
    g_rs = mm3(wr, ws)
    g_rr = mm3(wr, wr)
    for c in copies:
        c.wait()
    rs[...] = f_rs[...] - g_rs
    rs_a[...] = rs[: NS // 2, :]
    rs_b[...] = rs[NS // 2 :, :]
    rr = f_rr[...] - g_rr
    for n, (i, j) in enumerate(LOWER):
        rr_low[n] = rr[BLK * i : BLK * i + BLK, BLK * j : BLK * j + BLK]


def merge_a(mine, other, rs, lower, inv, v, work, next_block):
    for n, (i, j) in enumerate(LOWER):
        block = mine[n] + other[n]
        work[BLK * i : BLK * i + BLK, BLK * j : BLK * j + BLK] = block
        if i != j:
            work[BLK * j : BLK * j + BLK, BLK * i : BLK * i + BLK] = block.T
    v[...] = rs[...]
    factor(work, v, lower, inv, next_block)


def canonical(info, order):
    places = []
    for r in range(2):
        row_of = info.at[r : r + 1]
        sort_blocks(row_of, order)
        places += [row_of[0, order[KS + i]] for i in range(KS)]
    return [info[2, p - KS] for p in places]


def corner_blocks(low):
    blocks = {}
    for n, (i, j) in enumerate(LOWER):
        blocks[i, j] = low[n]
        if i != j:
            blocks[j, i] = low[n].T
    return blocks


def row_blocks(*parts):
    return [v.at[o : o + BLK, :] for v in parts for o in range(0, v.shape[0], BLK)]


def pair_update(rows, rr_low, spots, update, vs):
    where = ranks(spots)
    for e in range(KB):
        vs[at(BLK * where[e]), :] = rows[e][...]
    top, low = split(vs[0:NS, :]), split(vs[NS:, :])
    update[0:NS, 0:NS] = -mm3(top, top)
    update[NS:, 0:NS] = -mm3(low, top)
    update[NS:, NS:] = -mm3(low, low)
    for (i, j), block in corner_blocks(rr_low).items():
        r, c = at(BLK * where[i]), at(BLK * where[j])
        update[r, c] = update[r, c] + block


def merge_b(lower, inv, rs_other, v):
    v[...] = rs_other[...]
    solve(v, lower, inv)


def assemble_mine(lower, v_mine, v_first, v_second, rr_low, info, panel, update, vs, order):
    rows = row_blocks(v_mine, v_first, v_second)
    pair_update(rows, rr_low, canonical(info, order), update, vs)
    panel[0:NS, :] = lower[...]
    for r in range(2):
        row_of = info.at[r : r + 1]
        sort_blocks(row_of, order)
        for i in range(KS):
            panel[at(BLK * row_of[0, order[KS + i]]), :] = rows[KS * r + i][...]


def assemble_other(v_mine, v_first, v_second, rr_low, info, update, vs, order):
    pair_update(row_blocks(v_mine, v_first, v_second), rr_low, canonical(info, order), update, vs)


def last(up_a, up_b, low_a, low_b, info_a, info_b, panel, update, work, x, lower, inv, next_block, buf, order, sems):
    pairs = []
    for up, low, info in ((up_a, low_a, info_a), (up_b, low_b, info_b)):
        spots = canonical(info, order)
        pairs.append((up, corner_blocks(low), spots, ranks(spots)))
    work[...] = up_a[0:NS, 0:NS] + up_b[0:NS, 0:NS]
    for up, blocks, spots, where in pairs:
        for e in range(KB):

            @pl.when(where[e] >= KS)
            def _():
                x[at(BLK * (spots[e] - KS)), :] = up[at(BLK * where[e]), 0:NS]

        for (i, j), block in blocks.items():
            si, sj = spots[KS + i], spots[KS + j]

            @pl.when((si < KS) & (sj < KS))
            def _():
                r, c = at(BLK * si), at(BLK * sj)
                work[r, c] = work[r, c] + block

            @pl.when((si >= KS) & (sj < KS))
            def _():
                r, c = at(BLK * (si - KS)), at(BLK * sj)
                x[r, c] = x[r, c] + block

    factor(work, x, lower, inv, next_block)
    outs = [
        pltpu.make_async_copy(lower, panel.at[0:NS, :], sems.at[0]),
        pltpu.make_async_copy(x, panel.at[NS:, :], sems.at[1]),
    ]
    for c in outs:
        c.start()
    pair = split(x[...])
    for t in range(KB):
        rows = slice(BLK * t, BLK * t + BLK)
        buf[rows, :] = -mm3(tuple(p[rows] for p in pair), pair)
    for up, blocks, spots, where in pairs:
        for e in range(KB):
            for f in range(KB):

                @pl.when((where[e] >= KS) & (where[f] >= KS))
                def _():
                    r, c = at(BLK * (spots[e] - KS)), at(BLK * (spots[f] - KS))
                    add = up[at(BLK * where[e]), at(BLK * where[f])]
                    if e >= KS and f >= KS:
                        add = add + blocks[e - KS, f - KS]
                    buf[r, c] = buf[r, c] + add

    c = pltpu.make_async_copy(buf, update, sems.at[2])
    c.start()
    outs.append(c)
    for c in outs:
        c.wait()


def after(x, *earlier):
    return lax.optimization_barrier((x,) + earlier)[0]


def shards(leaf_front, place_pairs, place_quads):
    dma = pltpu.SemaphoreType.DMA
    tri = len(LOWER)
    half_cols = lax.axis_size("gx") // 2
    half_rows = lax.axis_size("gy") // 2

    def partner(x, axis):
        half = half_cols if axis == "gx" else half_rows
        return lax.ppermute(x, axis, [(i, (i + half) % (2 * half)) for i in range(2 * half)])

    pairs_other = partner(place_pairs, "gx")
    order = pltpu.SMEM((KB,), jnp.int32)

    corner, w = call(
        leaf_a, (sds(tri, BLK, BLK), sds(NB, NS)), [HBM, SMEM], [VMEM, VMEM],
        [pltpu.VMEM((NS, NS), f32), pltpu.VMEM((NS, NS), f32), pltpu.VMEM((KS, BLK, BLK), f32), pltpu.VMEM((BLK, BLK), f32),
         pltpu.VMEM((tri, BLK, BLK), f32), order, dma((1 + KB + tri,))],
        (leaf_front, place_pairs), 52)
    corner_other = partner(after(corner, pairs_other), "gx")
    half = NS // 2
    rs, rs_a, rs_b, rr_low = call(
        leaf_b, (sds(NS, NS), sds(half, NS), sds(half, NS), sds(tri, BLK, BLK)), [HBM, SMEM, VMEM], [VMEM] * 4,
        [pltpu.VMEM((NS, NS), f32), pltpu.VMEM((NS, NS), f32), order, dma((KS * KB,))],
        (leaf_front, place_pairs, w), 52)
    rr_far = partner(rr_low, "gy")
    info = jnp.concatenate([place_pairs, pairs_other, place_quads], 0)
    info_other = partner(info, "gy")
    corner, info_other = lax.optimization_barrier((corner, info_other))
    rs_first = partner(after(rs_a, corner_other), "gx")

    lower, inv, v_mine = call(
        merge_a, (sds(NS, NS), sds(KS, BLK, BLK), sds(NS, NS)), [VMEM] * 3, [VMEM] * 3,
        [pltpu.VMEM((NS, NS), f32), pltpu.VMEM((BLK, BLK), f32)], (corner, corner_other, rs))
    v_mine_far = partner(v_mine, "gy")
    rs_second = partner(after(rs_b, rs_first, lower, rr_far), "gx")
    v_first = call(merge_b, sds(half, NS), [VMEM] * 3, VMEM, [], (lower, inv, rs_first))
    v_first_far = partner(v_first, "gy")
    rr_other = partner(after(rr_low, rs_second, v_mine_far, v_first), "gx")
    v_second = call(merge_b, sds(half, NS), [VMEM] * 3, VMEM, [], (lower, inv, rs_second))
    v_second_far = partner(v_second, "gy")
    scratch = [pltpu.VMEM((NB, NS), f32), order]
    pair_panel, update = call(
        assemble_mine, (sds(NS + NB, NS), sds(NB, NB)), [VMEM] * 5 + [SMEM], [VMEM] * 2, scratch,
        (lower, v_mine, v_first, v_second, rr_low, info))
    rr_other_far = partner(after(rr_other, update, v_first_far, v_second_far), "gy")
    update_far = call(
        assemble_other, sds(NB, NB), [VMEM] * 4 + [SMEM], VMEM, scratch,
        (v_mine_far, v_first_far, v_second_far, rr_far, info_other))
    quad_panel, quad_update = call(
        last, (sds(NS + NB, NS), sds(NB, NB)), [VMEM] * 4 + [SMEM] * 2, [HBM, HBM],
        [pltpu.VMEM((NS, NS), f32), pltpu.VMEM((NB, NS), f32), pltpu.VMEM((NS, NS), f32),
         pltpu.VMEM((KS, BLK, BLK), f32), pltpu.VMEM((BLK, BLK), f32), pltpu.VMEM((NB, NB), f32), order, dma((3,))],
        (update, update_far, rr_other, rr_other_far, info, info_other))
    return pair_panel, quad_panel, quad_update


def solution(mesh):
    spec = P("gx", "gy")
    return jax.shard_map(
        shards, mesh=mesh, in_specs=(spec, spec, spec), out_specs=(spec, spec, spec), check_vma=False
    )
```

```python
import jax
import jax.numpy as jnp
from jax import lax
from jax.experimental import pallas as pl
from jax.experimental.pallas import tpu as pltpu
from jax.sharding import PartitionSpec as P

f32 = jnp.float32
bf16 = jnp.bfloat16
NT = (((1,), (1,)), ((), ()))
TN = (((0,), (0,)), ((), ()))
BLK = 128
KB = 8
KS = 4
NS = KS * BLK
NB = KB * BLK
NJ = NS + NB
BELOW = [(a, b) for a in range(KS) for b in range(a)]
PACKED = len(BELOW) + KS // 2
FIRST = PACKED - 3
VMEM = pl.BlockSpec(memory_space=pltpu.VMEM)
SMEM = pl.BlockSpec(memory_space=pltpu.SMEM)
HBM = pl.BlockSpec(memory_space=pltpu.HBM)


def sds(*shape):
    return jax.ShapeDtypeStruct(shape, f32)


def call(body, out, ins, outs, scratch, args, vmem=24, us=0):
    return pl.pallas_call(
        body,
        out_shape=out,
        in_specs=ins,
        out_specs=outs,
        scratch_shapes=scratch,
        cost_estimate=pl.CostEstimate(flops=1000, bytes_accessed=1000 + int(us * 3.5e6), transcendentals=0),
        compiler_params=pltpu.CompilerParams(vmem_limit_bytes=vmem * 1024 * 1024),
    )(*args)


def split(x):
    hi = x.astype(bf16)
    return hi, (x - hi.astype(f32)).astype(bf16)


def dot(a, b, dims):
    return lax.dot_general(a, b, dims, preferred_element_type=f32)


def mm3(a, b):
    return dot(jnp.concatenate([a[0], a[0], a[1]], 1), jnp.concatenate([b[0], b[1], b[0]], 1), NT)


def row(x, k):
    return jnp.broadcast_to(x[k : k + 1, :], x.shape)


def col(x, j):
    return jnp.broadcast_to(x[:, j : j + 1], (8, BLK))


def pack(blocks, out):
    ri = lax.broadcasted_iota(jnp.int32, (BLK, BLK), 0)
    ci = lax.broadcasted_iota(jnp.int32, (BLK, BLK), 1)
    for n, key in enumerate(BELOW):
        out(n, blocks[key])
    diagonals = []
    for n in range(KS // 2):
        one, two = blocks[2 * n, 2 * n], blocks[2 * n + 1, 2 * n + 1]
        out(len(BELOW) + n, jnp.where(ri >= ci, one, two))
        diagonals.append(jnp.sum(jnp.where(ri == ci, two, 0.0), axis=0, keepdims=True))
    return jnp.concatenate(diagonals + [jnp.zeros((8 - len(diagonals), BLK), f32)], 0)


def unpack(packed, tail):
    ri = lax.broadcasted_iota(jnp.int32, (BLK, BLK), 0)
    ci = lax.broadcasted_iota(jnp.int32, (BLK, BLK), 1)
    blocks = {}
    for n, block in packed.items():
        turned = block.T
        if n < len(BELOW):
            i, j = BELOW[n]
            blocks[i, j], blocks[j, i] = block, turned
        else:
            m = 2 * (n - len(BELOW))
            diagonal = jnp.broadcast_to(tail[m // 2 : m // 2 + 1, :], (BLK, BLK))
            blocks[m, m] = jnp.where(ri >= ci, block, turned)
            blocks[m + 1, m + 1] = jnp.where(ri < ci, block, jnp.where(ri > ci, turned, diagonal))
    return blocks


def rows_of(ref, first=0):
    return {first + n: ref[BLK * n : BLK * n + BLK, :] for n in range(ref.shape[0] // BLK)}


def unpack_all(ref):
    return unpack(rows_of(ref), ref[BLK * PACKED :, :])


def unpack_first(ref):
    return unpack(rows_of(ref), None)


def unpack_second(ref):
    return unpack(rows_of(ref, FIRST), ref[BLK * (PACKED - FIRST) :, :])


def factor_block(block):
    ri = lax.broadcasted_iota(jnp.int32, (8, BLK), 0)
    ci = lax.broadcasted_iota(jnp.int32, (8, BLK), 1)
    count, wide = BLK // 8, 4
    left = [block[8 * t : 8 * t + 8, :] for t in range(count)]
    right = [jnp.where(ci == ri + 8 * t, 1.0, 0.0).astype(f32) for t in range(count)]
    upper, inverse = [], []
    here = [col(left[0], k) for k in range(8)]
    for s in range(count):
        end = (s // wide + 1) * wide
        ahead = {w: [col(left[w], 8 * s + k) for k in range(8)] for w in range(s + 1, min(end + 1, count))}
        following = [col(left[s + 1], 8 * s + 8 + k) for k in range(8)] if s + 1 < count else None
        a, t = left[s], right[s]
        pivots = None
        for k in range(8):
            pivot = row(here[k], k)
            inv = pl.reciprocal(pivot, approx=True)
            pivots = pivot if k == 0 else jnp.where(ri == k, pivot, pivots)
            mult = jnp.where(ri > k, here[k], 0.0) * inv
            rows = {m: row(here[m], k) for m in range(k + 1, 8)}
            row_a, row_t = row(a, k), row(t, k)
            for m in range(k + 1, 8):
                here[m] = here[m] - mult * rows[m]
            a = a - mult * row_a
            t = t - mult * row_t
            for w, cols in ahead.items():
                mult = cols[k] * inv
                if w == s + 1:
                    following = [f - mult * row(cols[k], m) for m, f in enumerate(following)]
                for m in range(k + 1, 8):
                    cols[m] = cols[m] - mult * rows[m]
                left[w] = left[w] - mult * row_a
                right[w] = right[w] - mult * row_t
        here = following
        scale = lax.rsqrt(pivots)
        upper.append(a * scale)
        inverse.append(t * scale)
        if s + 1 == end and end + 1 < count:
            ah, al = split(jnp.concatenate(upper[-wide:], 0))
            th, tl = split(jnp.concatenate(inverse[-wide:], 0))
            lhs = jnp.concatenate([ah, ah, al], 0)
            rhs_a = jnp.concatenate([ah, al, ah], 0)
            rhs_t = jnp.concatenate([th, tl, th], 0)
            outer = dot(lhs, jnp.concatenate([rhs_a, rhs_t], 1), TN)
            for q in range(end + 1, count):
                left[q] = left[q] - outer[8 * q : 8 * q + 8, :BLK]
                right[q] = right[q] - outer[8 * q : 8 * q + 8, BLK:]
    return jnp.concatenate(inverse, 0)


def factor(work, x, lower, inv, corner, ready=None):
    ri = lax.broadcasted_iota(jnp.int32, (NS, BLK), 0)
    ci = lax.broadcasted_iota(jnp.int32, (NS, BLK), 1)

    def finish(k, inverse):
        here = at(BLK * k)
        inv[k] = inverse
        lower[:, here] = jnp.where(ri >= ci + BLK * k, mm3(split(work[:, here]), split(inverse)), 0.0)
        if not isinstance(k, int) or k + 1 < KS:
            then = at(BLK * jnp.minimum(k + 1, KS - 1))
            pair = split(lower[then, here])
            corner[...] = work[then, then] - mm3(pair, pair)

    def update(k):
        here = at(BLK * k)
        pair = split(lower[:, here])
        work[...] = work[...] - mm3(pair, pair)
        done = mm3(split(x[:, here]), split(inv[k]))
        x[...] = x[...] - mm3(split(done), pair)
        x[:, here] = done

    def step(k, carry):
        inverse = factor_block(corner[...])
        update(k - 1)
        finish(k, inverse)
        return carry

    inverse = factor_block(work[0:BLK, 0:BLK])
    if ready is not None:
        ready()
    finish(0, inverse)
    lax.fori_loop(1, KS, step, 0)
    x[:, NS - BLK :] = mm3(split(x[:, NS - BLK :]), split(inv[KS - 1]))


def solve(x, lower, inv):
    for k in range(KS):
        o, e = BLK * k, BLK * (k + 1)
        done = mm3(split(x[:, o:e]), split(inv[k]))
        x[:, o:e] = done
        if k + 1 < KS:
            x[:, e:] = x[:, e:] - mm3(split(done), split(lower[e:, o:e]))


def ranks(values):
    out = []
    for a, va in enumerate(values):
        r = jnp.int32(0)
        for b, vb in enumerate(values):
            if a != b:
                r = r + (vb < va).astype(jnp.int32)
        out.append(r)
    return out


def sort_blocks(place, order):
    values = [place[0, a] for a in range(KB)]
    for a, r in enumerate(ranks(values)):
        order[r] = jnp.int32(a)


def at(start):
    return pl.ds(pl.multiple_of(start, BLK), BLK)


def corner_of(ref):
    return {
        (i, j): ref[BLK * i : BLK * i + BLK, BLK * j : BLK * j + BLK] for i in range(KS) for j in range(i + 1)
    }


def leaf_a(front, place, corner, w_out, a, lower, inv, next_block, ss, order, sems):
    sort_blocks(place, order)
    copies = []
    for rows in (slice(0, BLK), slice(BLK, NS)):
        c = pltpu.make_async_copy(front.at[rows, 0:NS], a.at[rows, :], sems.at[len(copies)])
        c.start()
        copies.append(c)
    for t in range(KB):
        c = pltpu.make_async_copy(
            front.at[at(NS + BLK * order[t]), 0:NS], w_out.at[BLK * t : BLK * t + BLK, :], sems.at[len(copies)]
        )
        c.start()
        copies.append(c)
    for i in range(KS):
        for j in range(i + 1):
            c = pltpu.make_async_copy(
                front.at[at(NS + BLK * order[i]), at(NS + BLK * order[j])],
                ss.at[BLK * i : BLK * i + BLK, BLK * j : BLK * j + BLK],
                sems.at[len(copies)],
            )
            c.start()
            copies.append(c)
    copies[0].wait()

    def ready():
        for c in copies[1:]:
            c.wait()

    factor(a, w_out, lower, inv, next_block, ready)
    w = split(w_out[0:NS, :])
    gram = mm3(w, w)
    blocks = {}
    for i in range(KS):
        for j in range(i + 1):
            rows, cols = slice(BLK * i, BLK * i + BLK), slice(BLK * j, BLK * j + BLK)
            blocks[i, j] = ss[rows, cols] - gram[rows, cols]

    def out(n, block):
        corner[BLK * n : BLK * n + BLK, :] = block

    corner[BLK * PACKED :, :] = pack(blocks, out)


def leaf_b(front, place, w, rs, rr_all, rr_a, rr_b, f_rs, f_rr, order, sems):
    sort_blocks(place, order)
    copies = []
    for i in range(KS):
        for j in range(KB):
            dst = f_rs if j < KS else f_rr
            c = pltpu.make_async_copy(
                front.at[at(NS + BLK * order[KS + i]), at(NS + BLK * order[j])],
                dst.at[BLK * i : BLK * i + BLK, BLK * (j % KS) : BLK * (j % KS) + BLK],
                sems.at[i * KB + j],
            )
            c.start()
            copies.append(c)
    ws, wr = split(w[0:NS, :]), split(w[NS:, :])
    g_rs = mm3(wr, ws)
    g_rr = mm3(wr, wr)
    for c in copies:
        c.wait()
    rs[...] = f_rs[...] - g_rs
    f_rr[...] = f_rr[...] - g_rr

    def out(n, block):
        rr_all[BLK * n : BLK * n + BLK, :] = block
        if n < FIRST:
            rr_a[BLK * n : BLK * n + BLK, :] = block
        else:
            rr_b[BLK * (n - FIRST) : BLK * (n - FIRST) + BLK, :] = block

    tail = pack(corner_of(f_rr), out)
    rr_all[BLK * PACKED :, :] = tail
    rr_b[BLK * (PACKED - FIRST) :, :] = tail


def merge_a(mine, other, rs, lower, inv, v, work, next_block):
    packed = {n: block + other[BLK * n : BLK * n + BLK, :] for n, block in rows_of(mine).items()}
    tail = mine[BLK * PACKED :, :] + other[BLK * PACKED :, :]
    for (i, j), block in unpack(packed, tail).items():
        work[BLK * i : BLK * i + BLK, BLK * j : BLK * j + BLK] = block
    v[...] = rs[...]
    factor(work, v, lower, inv, next_block)


def canonical(info, order):
    places = []
    for r in range(2):
        row_of = info.at[r : r + 1]
        sort_blocks(row_of, order)
        places += [row_of[0, order[KS + i]] for i in range(KS)]
    return [info[2, p - KS] for p in places]


def row_blocks(*parts):
    return [v.at[o : o + BLK, :] for v in parts for o in range(0, v.shape[0], BLK)]


def pair_update(rows, rr_low, spots, update, vs):
    where = ranks(spots)
    for e in range(KB):
        vs[at(BLK * where[e]), :] = rows[e][...]
    top, low = split(vs[0:NS, :]), split(vs[NS:, :])
    update[0:NS, 0:NS] = -mm3(top, top)
    update[NS:, 0:NS] = -mm3(low, top)
    update[NS:, NS:] = -mm3(low, low)
    for (i, j), block in unpack_all(rr_low).items():
        r, c = at(BLK * where[i]), at(BLK * where[j])
        update[r, c] = update[r, c] + block


def merge_b(lower, inv, rs_other, v):
    v[...] = rs_other[...]
    solve(v, lower, inv)


def assemble_mine(lower, v_mine, v_other, rr_low, info, panel, update, vs, order):
    rows = row_blocks(v_mine, v_other)
    pair_update(rows, rr_low, canonical(info, order), update, vs)
    panel[0:NS, :] = lower[...]
    for r in range(2):
        row_of = info.at[r : r + 1]
        sort_blocks(row_of, order)
        for i in range(KS):
            panel[at(BLK * row_of[0, order[KS + i]]), :] = rows[KS * r + i][...]


def assemble_other(v_mine, v_other, rr_low, info, update, vs, order):
    pair_update(row_blocks(v_mine, v_other), rr_low, canonical(info, order), update, vs)


def add_blocks(blocks, spots, ss, x, rr):
    for (i, j), block in blocks.items():
        si, sj = spots[i], spots[j]

        @pl.when((si < KS) & (sj < KS))
        def _():
            r, c = at(BLK * si), at(BLK * sj)
            ss[r, c] = ss[r, c] + block

        @pl.when((si >= KS) & (sj < KS))
        def _():
            r, c = at(BLK * (si - KS)), at(BLK * sj)
            x[r, c] = x[r, c] + block

        @pl.when((si >= KS) & (sj >= KS))
        def _():
            r, c = at(BLK * (si - KS)), at(BLK * (sj - KS))
            rr[r, c] = rr[r, c] + block


def join(up_a, up_b, low_a1, low_a2, low_b1, info_a, info_b, ss, x, rr, order):
    ss[...] = up_a[0:NS, 0:NS] + up_b[0:NS, 0:NS]
    rr[...] = jnp.zeros((NB, NB), f32)
    far = []
    for up, info in ((up_a, info_a), (up_b, info_b)):
        spots = canonical(info, order)
        far.append(spots[KS:])
        for spot, rank in zip(spots, ranks(spots)):
            order[rank] = spot
        for i in range(KS):
            r = at(BLK * (order[KS + i] - KS))
            rows = slice(NS + BLK * i, NS + BLK * i + BLK)
            x[r, :] = up[rows, 0:NS]
            for j in range(KS):
                rr[r, at(BLK * (order[KS + j] - KS))] = up[rows, NS + BLK * j : NS + BLK * j + BLK]
    add_blocks(unpack_first(low_a1), far[0], ss, x, rr)
    add_blocks(unpack_second(low_a2), far[0], ss, x, rr)
    add_blocks(unpack_first(low_b1), far[1], ss, x, rr)


def last(ss, x_in, rr, low, info, panel, update, work, x, lower, inv, next_block, buf, order, sems):
    fill = pltpu.make_async_copy(rr, buf, sems.at[0])
    fill.start()
    work[...] = ss[...]
    x[...] = x_in[...]
    far = canonical(info, order)[KS:]
    blocks = unpack_second(low)
    fill.wait()
    add_blocks(blocks, far, work, x, buf)
    factor(work, x, lower, inv, next_block)
    outs = [
        pltpu.make_async_copy(lower, panel.at[0:NS, :], sems.at[1]),
        pltpu.make_async_copy(x, panel.at[NS:, :], sems.at[2]),
    ]
    for c in outs:
        c.start()
    pair = split(x[...])
    wide = 2 * BLK
    for t in range(NB // wide):
        cols = slice(wide * t, wide * t + wide)
        buf[:, cols] = buf[:, cols] - mm3(pair, tuple(p[cols] for p in pair))
        c = pltpu.make_async_copy(buf.at[:, cols], update.at[:, cols], sems.at[3 + t])
        c.start()
        outs.append(c)
    for c in outs:
        c.wait()


def after(x, *earlier):
    return lax.optimization_barrier((x,) + earlier)[0]


def shards(leaf_front, place_pairs, place_quads):
    dma = pltpu.SemaphoreType.DMA
    half_cols = lax.axis_size("gx") // 2
    half_rows = lax.axis_size("gy") // 2

    def partner(x, axis):
        half = half_cols if axis == "gx" else half_rows
        return lax.ppermute(x, axis, [(i, (i + half) % (2 * half)) for i in range(2 * half)])

    def vmem(*shape):
        return pltpu.VMEM(shape, f32)

    order = pltpu.SMEM((KB,), jnp.int32)
    factor_scratch = [vmem(NS, NS), vmem(KS, BLK, BLK), vmem(BLK, BLK)]
    tri = sds(BLK * PACKED + 8, BLK)
    tri_a, tri_b = sds(BLK * FIRST, BLK), sds(BLK * (PACKED - FIRST) + 8, BLK)

    pairs_other = partner(place_pairs, "gx")
    corner, w = call(
        leaf_a, (tri, sds(NB, NS)), [HBM, SMEM], [VMEM, VMEM],
        [vmem(NS, NS)] + factor_scratch + [vmem(NS, NS), order, dma((2 + KB + KS * (KS + 1) // 2,))],
        (leaf_front, place_pairs), 48)
    corner_other = partner(after(corner, pairs_other), "gx")
    rs, rr, rr_a, rr_b = call(
        leaf_b, (sds(NS, NS), tri, tri_a, tri_b), [HBM, SMEM, VMEM], [VMEM] * 4,
        [vmem(NS, NS), vmem(NS, NS), order, dma((KS * KB,))], (leaf_front, place_pairs, w), 48)
    rr_far = partner(rr, "gy")
    info = jnp.concatenate([place_pairs, pairs_other, place_quads], 0)
    info_other = partner(info, "gy")
    corner, info_other = lax.optimization_barrier((corner, info_other))
    rs_other = partner(after(rs, corner_other), "gx")

    lower, inv, v_mine = call(
        merge_a, (sds(NS, NS), sds(KS, BLK, BLK), sds(NS, NS)), [VMEM] * 3, [VMEM] * 3,
        [vmem(NS, NS), vmem(BLK, BLK)], (corner, corner_other, rs), us=13)
    v_mine_far = partner(after(v_mine, rr_far), "gy")
    rr_first = partner(after(rr_a, v_mine_far), "gx")
    v_other = call(merge_b, sds(NS, NS), [VMEM] * 3, VMEM, [], (lower, inv, rs_other))
    v_other_far = partner(v_other, "gy")
    scratch = [vmem(NB, NS), order]
    pair_panel, update = call(
        assemble_mine, (sds(NS + NB, NS), sds(NB, NB)), [VMEM] * 4 + [SMEM], [VMEM] * 2, scratch,
        (lower, v_mine, v_other, rr, info))
    rr_first, update = lax.optimization_barrier((rr_first, update))
    rr_second = partner(after(rr_b, rr_first), "gx")
    rr_first_far = partner(rr_first, "gy")
    update_far = call(
        assemble_other, sds(NB, NB), [VMEM] * 3 + [SMEM], VMEM, scratch,
        (v_mine_far, v_other_far, rr_far, info_other))
    rr_second_far = partner(after(rr_second, update_far, rr_first_far), "gy")
    ss, x, rr = call(
        join, (sds(NS, NS), sds(NB, NS), sds(NB, NB)), [VMEM] * 5 + [SMEM] * 2, [VMEM] * 3, [order],
        (update, update_far, rr_first, rr_second, rr_first_far, info, info_other))
    quad_panel, quad_update = call(
        last, (sds(NS + NB, NS), sds(NB, NB)), [VMEM] * 4 + [SMEM], [HBM, HBM],
        [vmem(NS, NS), vmem(NB, NS)] + factor_scratch + [vmem(NB, NB), order, dma((3 + KB,))],
        (ss, x, rr, rr_second_far, info_other))
    return pair_panel, quad_panel, quad_update


def solution(mesh):
    spec = P("gx", "gy")
    return jax.shard_map(
        shards, mesh=mesh, in_specs=(spec, spec, spec), out_specs=(spec, spec, spec), check_vma=False
    )
```

```python
import jax
import jax.numpy as jnp
from jax import lax
from jax.experimental import pallas as pl
from jax.experimental.pallas import tpu as pltpu
from jax.sharding import PartitionSpec as P

f32 = jnp.float32
bf16 = jnp.bfloat16
NT = (((1,), (1,)), ((), ()))
TN = (((0,), (0,)), ((), ()))
BLK = 128
KB = 8
KS = 4
NS = KS * BLK
NB = KB * BLK
NJ = NS + NB
BELOW = [(a, b) for a in range(KS) for b in range(a)]
PACKED = len(BELOW) + KS // 2
FIRST = PACKED - 2
PLACE_ROW = BLK * PACKED + KS // 2
VMEM = pl.BlockSpec(memory_space=pltpu.VMEM)
SMEM = pl.BlockSpec(memory_space=pltpu.SMEM)
HBM = pl.BlockSpec(memory_space=pltpu.HBM)


def sds(*shape):
    return jax.ShapeDtypeStruct(shape, f32)


def call(body, out, ins, outs, scratch, args, vmem=24, us=0):
    return pl.pallas_call(
        body,
        out_shape=out,
        in_specs=ins,
        out_specs=outs,
        scratch_shapes=scratch,
        cost_estimate=pl.CostEstimate(flops=1000, bytes_accessed=1000 + int(us * 3.5e6), transcendentals=0),
        compiler_params=pltpu.CompilerParams(vmem_limit_bytes=vmem * 1024 * 1024),
    )(*args)


def split(x):
    hi = x.astype(bf16)
    return hi, (x - hi.astype(f32)).astype(bf16)


def dot(a, b, dims):
    return lax.dot_general(a, b, dims, preferred_element_type=f32)


def mm3(a, b):
    return dot(jnp.concatenate([a[0], a[0], a[1]], 1), jnp.concatenate([b[0], b[1], b[0]], 1), NT)


def row(x, k):
    return jnp.broadcast_to(x[k : k + 1, :], x.shape)


def col(x, j):
    return jnp.broadcast_to(x[:, j : j + 1], (8, BLK))


def pack(blocks, out):
    ri = lax.broadcasted_iota(jnp.int32, (BLK, BLK), 0)
    ci = lax.broadcasted_iota(jnp.int32, (BLK, BLK), 1)
    for n, key in enumerate(BELOW):
        out(n, blocks[key])
    diagonals = []
    for n in range(KS // 2):
        one, two = blocks[2 * n, 2 * n], blocks[2 * n + 1, 2 * n + 1]
        out(len(BELOW) + n, jnp.where(ri >= ci, one, two))
        diagonals.append(jnp.sum(jnp.where(ri == ci, two, 0.0), axis=0, keepdims=True))
    return jnp.concatenate(diagonals + [jnp.zeros((8 - len(diagonals), BLK), f32)], 0)


def unpack(packed, tail):
    ri = lax.broadcasted_iota(jnp.int32, (BLK, BLK), 0)
    ci = lax.broadcasted_iota(jnp.int32, (BLK, BLK), 1)
    blocks = {}
    for n, block in packed.items():
        turned = block.T
        if n < len(BELOW):
            i, j = BELOW[n]
            blocks[i, j], blocks[j, i] = block, turned
        else:
            m = 2 * (n - len(BELOW))
            diagonal = jnp.broadcast_to(tail[m // 2 : m // 2 + 1, :], (BLK, BLK))
            blocks[m, m] = jnp.where(ri >= ci, block, turned)
            blocks[m + 1, m + 1] = jnp.where(ri < ci, block, jnp.where(ri > ci, turned, diagonal))
    return blocks


def rows_of(ref, first=0):
    return {first + n: ref[BLK * n : BLK * n + BLK, :] for n in range(ref.shape[0] // BLK)}


def unpack_all(ref):
    return unpack(rows_of(ref), ref[BLK * PACKED :, :])


def unpack_first(ref):
    return unpack(rows_of(ref), None)


def unpack_second(ref):
    return unpack(rows_of(ref, FIRST), ref[BLK * (PACKED - FIRST) :, :])


def factor_block(block):
    ri = lax.broadcasted_iota(jnp.int32, (8, BLK), 0)
    ci = lax.broadcasted_iota(jnp.int32, (8, BLK), 1)
    count, wide = BLK // 8, 4
    left = [block[8 * t : 8 * t + 8, :] for t in range(count)]
    right = [jnp.where(ci == ri + 8 * t, 1.0, 0.0).astype(f32) for t in range(count)]
    upper, inverse = [], []
    here = [col(left[0], k) for k in range(8)]
    for s in range(count):
        end = (s // wide + 1) * wide
        ahead = {w: [col(left[w], 8 * s + k) for k in range(8)] for w in range(s + 1, min(end + 1, count))}
        following = [col(left[s + 1], 8 * s + 8 + k) for k in range(8)] if s + 1 < count else None
        a, t = left[s], right[s]
        pivots = None
        for k in range(8):
            pivot = row(here[k], k)
            inv = pl.reciprocal(pivot, approx=True)
            pivots = pivot if k == 0 else jnp.where(ri == k, pivot, pivots)
            mult = jnp.where(ri > k, here[k], 0.0) * inv
            rows = {m: row(here[m], k) for m in range(k + 1, 8)}
            row_a, row_t = row(a, k), row(t, k)
            for m in range(k + 1, 8):
                here[m] = here[m] - mult * rows[m]
            a = a - mult * row_a
            t = t - mult * row_t
            for w, cols in ahead.items():
                mult = cols[k] * inv
                if w == s + 1:
                    following = [f - mult * row(cols[k], m) for m, f in enumerate(following)]
                for m in range(k + 1, 8):
                    cols[m] = cols[m] - mult * rows[m]
                left[w] = left[w] - mult * row_a
                right[w] = right[w] - mult * row_t
        here = following
        scale = lax.rsqrt(pivots)
        upper.append(a * scale)
        inverse.append(t * scale)
        if s + 1 == end and end + 1 < count:
            ah, al = split(jnp.concatenate(upper[-wide:], 0))
            th, tl = split(jnp.concatenate(inverse[-wide:], 0))
            lhs = jnp.concatenate([ah, ah, al], 0)
            rhs_a = jnp.concatenate([ah, al, ah], 0)
            rhs_t = jnp.concatenate([th, tl, th], 0)
            outer = dot(lhs, jnp.concatenate([rhs_a, rhs_t], 1), TN)
            for q in range(end + 1, count):
                left[q] = left[q] - outer[8 * q : 8 * q + 8, :BLK]
                right[q] = right[q] - outer[8 * q : 8 * q + 8, BLK:]
    return jnp.concatenate(inverse, 0)


def factor(work, x, lower, inv, corner, gram=None, ready=None):
    ri = lax.broadcasted_iota(jnp.int32, (NS, BLK), 0)
    ci = lax.broadcasted_iota(jnp.int32, (NS, BLK), 1)

    def finish(k, inverse):
        here, then = at(BLK * k), at(BLK * jnp.minimum(k + 1, KS - 1))
        inv[k] = inverse
        pair = split(mm3(split(work[then, here]), split(inverse)))
        corner[...] = work[then, then] - mm3(pair, pair)

    def column(k):
        here = at(BLK * k)
        inverse = split(inv[k])
        panel = jnp.where(ri >= ci + BLK * k, mm3(split(work[:, here]), inverse), 0.0)
        lower[:, here] = panel
        return here, split(panel), mm3(split(x[:, here]), inverse)

    def update(k):
        here, pair, done = column(k)
        work[...] = work[...] - mm3(pair, pair)
        new = split(done)
        x[...] = x[...] - mm3(new, pair)
        x[:, here] = done
        if gram is not None:
            top = tuple(v[: gram.shape[0]] for v in new)
            gram[...] = gram[...] - mm3(top, top)

    def step(k, carry):
        inverse = factor_block(corner[...])
        update(k - 1)
        finish(k, inverse)
        return carry

    inverse = factor_block(work[0:BLK, 0:BLK])
    if ready is not None:
        ready()
    finish(0, inverse)
    lax.fori_loop(1, KS, step, 0)
    here, _, done = column(KS - 1)
    x[:, here] = done


def solve(x, lower, inv):
    for k in range(KS):
        o, e = BLK * k, BLK * (k + 1)
        done = mm3(split(x[:, o:e]), split(inv[k]))
        x[:, o:e] = done
        if k + 1 < KS:
            x[:, e:] = x[:, e:] - mm3(split(done), split(lower[e:, o:e]))


def ranks(values):
    out = []
    for a, va in enumerate(values):
        r = jnp.int32(0)
        for b, vb in enumerate(values):
            if a != b:
                r = r + (vb < va).astype(jnp.int32)
        out.append(r)
    return out


def sort_blocks(place, order):
    values = [place[0, a] for a in range(KB)]
    for a, r in enumerate(ranks(values)):
        order[r] = jnp.int32(a)


def at(start):
    return pl.ds(pl.multiple_of(start, BLK), BLK)


def corner_of(ref):
    return {
        (i, j): ref[BLK * i : BLK * i + BLK, BLK * j : BLK * j + BLK] for i in range(KS) for j in range(i + 1)
    }


def leaf_a(front, place_in, corner, w_out, lower, inv, a, next_block, ss, place, order, sems):
    copies = []
    for rows in (slice(0, BLK), slice(BLK, NS)):
        c = pltpu.make_async_copy(front.at[rows, 0:NS], a.at[rows, :], sems.at[len(copies)])
        c.start()
        copies.append(c)
    c = pltpu.make_async_copy(place_in, place, sems.at[len(copies)])
    c.start()
    c.wait()
    sort_blocks(place, order)
    for t in range(KS):
        c = pltpu.make_async_copy(
            front.at[at(NS + BLK * order[t]), 0:NS], w_out.at[BLK * t : BLK * t + BLK, :], sems.at[1 + len(copies)]
        )
        c.start()
        copies.append(c)
    for i in range(KS):
        for j in range(i + 1):
            c = pltpu.make_async_copy(
                front.at[at(NS + BLK * order[i]), at(NS + BLK * order[j])],
                ss.at[BLK * i : BLK * i + BLK, BLK * j : BLK * j + BLK],
                sems.at[1 + len(copies)],
            )
            c.start()
            copies.append(c)
    copies[0].wait()

    def ready():
        for c in copies[1:]:
            c.wait()

    factor(a, w_out, lower, inv, next_block, ss, ready)
    w = split(w_out[:, NS - BLK :])
    gram = mm3(w, w)
    blocks = {}
    for i in range(KS):
        for j in range(i + 1):
            rows, cols = slice(BLK * i, BLK * i + BLK), slice(BLK * j, BLK * j + BLK)
            blocks[i, j] = ss[rows, cols] - gram[rows, cols]

    def out(n, block):
        corner[BLK * n : BLK * n + BLK, :] = block

    corner[BLK * PACKED :, :] = pack(blocks, out)
    lane = lax.broadcasted_iota(jnp.int32, (1, BLK), 1)
    places = jnp.zeros((1, BLK), f32)
    for b in range(KB):
        places = jnp.where(lane == b, place[0, b].astype(f32), places)
    corner[PLACE_ROW : PLACE_ROW + 1, :] = places


def leaf_b(front, place_in, w, lower, inv, rs, rr_all, rr_a, rr_b, wr, f_rs, f_rr, place, order, sems):
    c = pltpu.make_async_copy(place_in, place, sems.at[KS * KB])
    c.start()
    c.wait()
    sort_blocks(place, order)
    copies = []
    for i in range(KS):
        c = pltpu.make_async_copy(
            front.at[at(NS + BLK * order[KS + i]), 0:NS], wr.at[BLK * i : BLK * i + BLK, :], sems.at[KS * KB + 1 + i]
        )
        c.start()
        copies.append(c)
    for i in range(KS):
        for j in range(KB):
            dst = f_rs if j < KS else f_rr
            c = pltpu.make_async_copy(
                front.at[at(NS + BLK * order[KS + i]), at(NS + BLK * order[j])],
                dst.at[BLK * i : BLK * i + BLK, BLK * (j % KS) : BLK * (j % KS) + BLK],
                sems.at[i * KB + j],
            )
            c.start()
            copies.append(c)
    for c in copies[:KS]:
        c.wait()
    solve(wr, lower, inv)
    ws, wr_pair = split(w[...]), split(wr[...])
    g_rs = mm3(wr_pair, ws)
    g_rr = mm3(wr_pair, wr_pair)
    for c in copies[KS:]:
        c.wait()
    rs[...] = f_rs[...] - g_rs
    f_rr[...] = f_rr[...] - g_rr

    def out(n, block):
        rr_all[BLK * n : BLK * n + BLK, :] = block
        if n < FIRST:
            rr_a[BLK * n : BLK * n + BLK, :] = block
        else:
            rr_b[BLK * (n - FIRST) : BLK * (n - FIRST) + BLK, :] = block

    tail = pack(corner_of(f_rr), out)
    rr_all[BLK * PACKED :, :] = tail
    rr_b[BLK * (PACKED - FIRST) :, :] = tail


def merge_a(mine, other, rs, lower, inv, v, work, next_block):
    packed = {n: block + other[BLK * n : BLK * n + BLK, :] for n, block in rows_of(mine).items()}
    tail = mine[BLK * PACKED :, :] + other[BLK * PACKED :, :]
    for (i, j), block in unpack(packed, tail).items():
        work[BLK * i : BLK * i + BLK, BLK * j : BLK * j + BLK] = block
    v[...] = rs[...]
    factor(work, v, lower, inv, next_block)


def canonical(info, order):
    places = []
    for r in range(2):
        row_of = info.at[r : r + 1]
        sort_blocks(row_of, order)
        places += [row_of[0, order[KS + i]] for i in range(KS)]
    return [info[2, p - KS] for p in places]


def row_blocks(*parts):
    return [v.at[o : o + BLK, :] for v in parts for o in range(0, v.shape[0], BLK)]


def pair_update(rows, rr_low, spots, update, vs):
    where = ranks(spots)
    for e in range(KB):
        vs[at(BLK * where[e]), :] = rows[e][...]
    top, low = split(vs[0:NS, :]), split(vs[NS:, :])
    update[0:NS, 0:NS] = -mm3(top, top)
    update[NS:, 0:NS] = -mm3(low, top)
    update[NS:, NS:] = -mm3(low, low)
    for (i, j), block in unpack_all(rr_low).items():
        r, c = at(BLK * where[i]), at(BLK * where[j])
        update[r, c] = update[r, c] + block


def merge_b(lower, inv, rs_other, v):
    v[...] = rs_other[...]
    solve(v, lower, inv)


def assemble_mine(lower, v_mine, v_other, rr_low, info, panel, update, vs, order):
    rows = row_blocks(v_mine, v_other)
    pair_update(rows, rr_low, canonical(info, order), update, vs)
    panel[0:NS, :] = lower[...]
    for r in range(2):
        row_of = info.at[r : r + 1]
        sort_blocks(row_of, order)
        for i in range(KS):
            panel[at(BLK * row_of[0, order[KS + i]]), :] = rows[KS * r + i][...]


def assemble_other(v_mine, v_other, rr_low, info, update, vs, order):
    pair_update(row_blocks(v_mine, v_other), rr_low, canonical(info, order), update, vs)


def add_blocks(blocks, spots, ss=None, x=None, rr=None):
    for (i, j), block in blocks.items():
        si, sj = spots[i], spots[j]

        def add(part, cond, r, c):
            if part is not None:

                @pl.when(cond)
                def _():
                    part[at(BLK * r), at(BLK * c)] = part[at(BLK * r), at(BLK * c)] + block

        add(ss, (si < KS) & (sj < KS), si, sj)
        add(x, (si >= KS) & (sj < KS), si - KS, sj)
        add(rr, (si >= KS) & (sj >= KS), si - KS, sj - KS)


def join(up_a, up_b, low_a1, low_a2, low_b1, info_a, info_b, ss, x, rr, order):
    ss[...] = up_a[0:NS, 0:NS] + up_b[0:NS, 0:NS]
    rr[...] = jnp.zeros((NB, NB), f32)
    far = []
    for up, info in ((up_a, info_a), (up_b, info_b)):
        spots = canonical(info, order)
        far.append(spots[KS:])
        for spot, rank in zip(spots, ranks(spots)):
            order[rank] = spot
        for i in range(KS):
            r = at(BLK * (order[KS + i] - KS))
            rows = slice(NS + BLK * i, NS + BLK * i + BLK)
            x[r, :] = up[rows, 0:NS]
            for j in range(KS):
                rr[r, at(BLK * (order[KS + j] - KS))] = up[rows, NS + BLK * j : NS + BLK * j + BLK]
    add_blocks(unpack_first(low_a1), far[0], ss, x, rr)
    add_blocks(unpack_second(low_a2), far[0], ss, x, rr)
    add_blocks(unpack_first(low_b1), far[1], ss, x, rr)


def last(ss, x_in, rr, low, info, panel, update, work, x, lower, inv, next_block, buf, order, sems):
    fill = pltpu.make_async_copy(rr, buf, sems.at[0])
    fill.start()
    work[...] = ss[...]
    x[...] = x_in[...]
    far = canonical(info, order)[KS:]
    add_blocks(unpack_second(low), far, ss=work, x=x)

    factor(work, x, lower, inv, next_block)
    outs = [
        pltpu.make_async_copy(lower, panel.at[0:NS, :], sems.at[1]),
        pltpu.make_async_copy(x, panel.at[NS:, :], sems.at[2]),
    ]
    for c in outs:
        c.start()
    fill.wait()
    add_blocks(unpack_second(low), far, rr=buf)
    pair = split(x[...])
    wide = 2 * BLK
    for t in range(NB // wide):
        o, e = wide * t, wide * t + wide
        product = mm3(tuple(p[o:] for p in pair), tuple(p[o:e] for p in pair))
        buf[o:, o:e] = buf[o:, o:e] - product
        if e < NB:
            buf[o:e, e:] = buf[o:e, e:] - product[wide:].T
        c = pltpu.make_async_copy(buf.at[:, o:e], update.at[:, o:e], sems.at[3 + t])
        c.start()
        outs.append(c)
    for c in outs:
        c.wait()


def after(x, *earlier):
    return lax.optimization_barrier((x,) + earlier)[0]


def shards(leaf_front, place_pairs, place_quads):
    dma = pltpu.SemaphoreType.DMA
    half_cols = lax.axis_size("gx") // 2
    half_rows = lax.axis_size("gy") // 2

    def partner(x, axis):
        half = half_cols if axis == "gx" else half_rows
        return lax.ppermute(x, axis, [(i, (i + half) % (2 * half)) for i in range(2 * half)])

    def vmem(*shape):
        return pltpu.VMEM(shape, f32)

    order = pltpu.SMEM((KB,), jnp.int32)
    factor_scratch = [vmem(NS, NS), vmem(KS, BLK, BLK), vmem(BLK, BLK)]
    tri = sds(BLK * PACKED + 8, BLK)
    tri_a, tri_b = sds(BLK * FIRST, BLK), sds(BLK * (PACKED - FIRST) + 8, BLK)

    place = pltpu.SMEM((1, KB), jnp.int32)
    corner, w, lower, inv = call(
        leaf_a, (tri, sds(NS, NS), sds(NS, NS), sds(KS, BLK, BLK)), [HBM, HBM], [VMEM] * 4,
        [vmem(NS, NS), vmem(BLK, BLK), vmem(NS, NS), place, order, dma((3 + KS + KS * (KS + 1) // 2,))],
        (leaf_front, place_pairs), 48)
    corner_other = partner(corner, "gx")
    rs, rr, rr_a, rr_b = call(
        leaf_b, (sds(NS, NS), tri, tri_a, tri_b), [HBM, HBM, VMEM, VMEM, VMEM], [VMEM] * 4,
        [vmem(NS, NS), vmem(NS, NS), vmem(NS, NS), place, order, dma((KS * KB + 1 + KS,))],
        (leaf_front, place_pairs, w, lower, inv), 48)
    rr_far = partner(rr, "gy")
    rs_other = partner(after(rs, corner_other), "gx")

    lower, inv, v_mine = call(
        merge_a, (sds(NS, NS), sds(KS, BLK, BLK), sds(NS, NS)), [VMEM] * 3, [VMEM] * 3,
        [vmem(NS, NS), vmem(BLK, BLK)], (corner, corner_other, rs), us=13)
    v_mine_far = partner(after(v_mine, rr_far), "gy")
    pairs_other = corner_other[PLACE_ROW : PLACE_ROW + 1, :KB].astype(jnp.int32)
    info = jnp.concatenate([place_pairs, pairs_other, place_quads], 0)
    info_other = partner(after(info, lower), "gy")
    rs_other, info_other = lax.optimization_barrier((rs_other, info_other))
    rr_first = partner(after(rr_a, v_mine_far), "gx")
    v_other = call(merge_b, sds(NS, NS), [VMEM] * 3, VMEM, [], (lower, inv, rs_other))
    v_other_far = partner(v_other, "gy")
    scratch = [vmem(NB, NS), order]
    pair_panel, update = call(
        assemble_mine, (sds(NS + NB, NS), sds(NB, NB)), [VMEM] * 4 + [SMEM], [VMEM] * 2, scratch,
        (lower, v_mine, v_other, rr, info))
    rr_first, update = lax.optimization_barrier((rr_first, update))
    rr_second = partner(after(rr_b, rr_first), "gx")
    rr_first_far = partner(rr_first, "gy")
    update_far = call(
        assemble_other, sds(NB, NB), [VMEM] * 3 + [SMEM], VMEM, scratch,
        (v_mine_far, v_other_far, rr_far, info_other))
    rr_second_far = partner(after(rr_second, update_far), "gy")
    ss, x, rr = call(
        join, (sds(NS, NS), sds(NB, NS), sds(NB, NB)), [VMEM] * 5 + [SMEM] * 2, [VMEM] * 3, [order],
        (update, update_far, rr_first, rr_second, rr_first_far, info, info_other))
    quad_panel, quad_update = call(
        last, (sds(NS + NB, NS), sds(NB, NB)), [VMEM] * 4 + [SMEM], [HBM, HBM],
        [vmem(NS, NS), vmem(NB, NS)] + factor_scratch + [vmem(NB, NB), order, dma((3 + KB,))],
        (ss, x, rr, rr_second_far, info_other))
    return pair_panel, quad_panel, quad_update


def solution(mesh):
    spec = P("gx", "gy")
    return jax.shard_map(
        shards, mesh=mesh, in_specs=(spec, spec, spec), out_specs=(spec, spec, spec), check_vma=False
    )
```

```python
import jax
import jax.numpy as jnp
from jax import lax
from jax.experimental import pallas as pl
from jax.experimental.pallas import tpu as pltpu
from jax.sharding import PartitionSpec as P

f32 = jnp.float32
bf16 = jnp.bfloat16
NT = (((1,), (1,)), ((), ()))
TN = (((0,), (0,)), ((), ()))
BLK = 128
KB = 8
KS = 4
NS = KS * BLK
NB = KB * BLK
NJ = NS + NB
BELOW = [(a, b) for a in range(KS) for b in range(a)]
PACKED = len(BELOW) + KS // 2
FIRST = PACKED - 2
PLACE_ROW = BLK * PACKED + KS // 2
VMEM = pl.BlockSpec(memory_space=pltpu.VMEM)
SMEM = pl.BlockSpec(memory_space=pltpu.SMEM)
HBM = pl.BlockSpec(memory_space=pltpu.HBM)


def sds(*shape):
    return jax.ShapeDtypeStruct(shape, f32)


def call(body, out, ins, outs, scratch, args, vmem=24, us=0):
    return pl.pallas_call(
        body,
        out_shape=out,
        in_specs=ins,
        out_specs=outs,
        scratch_shapes=scratch,
        cost_estimate=pl.CostEstimate(flops=1000, bytes_accessed=1000 + int(us * 3.5e6), transcendentals=0),
        compiler_params=pltpu.CompilerParams(vmem_limit_bytes=vmem * 1024 * 1024),
    )(*args)


def split(x):
    hi = x.astype(bf16)
    return hi, (x - hi.astype(f32)).astype(bf16)


def dot(a, b, dims):
    return lax.dot_general(a, b, dims, preferred_element_type=f32)


def mm3(a, b):
    return dot(jnp.concatenate([a[0], a[0], a[1]], 1), jnp.concatenate([b[0], b[1], b[0]], 1), NT)


def row(x, k):
    return jnp.broadcast_to(x[k : k + 1, :], x.shape)


def col(x, j):
    return jnp.broadcast_to(x[:, j : j + 1], (8, BLK))


def pack(blocks, out):
    ri = lax.broadcasted_iota(jnp.int32, (BLK, BLK), 0)
    ci = lax.broadcasted_iota(jnp.int32, (BLK, BLK), 1)
    for n, key in enumerate(BELOW):
        out(n, blocks[key])
    diagonals = []
    for n in range(KS // 2):
        one, two = blocks[2 * n, 2 * n], blocks[2 * n + 1, 2 * n + 1]
        out(len(BELOW) + n, jnp.where(ri >= ci, one, two))
        diagonals.append(jnp.sum(jnp.where(ri == ci, two, 0.0), axis=0, keepdims=True))
    return jnp.concatenate(diagonals + [jnp.zeros((8 - len(diagonals), BLK), f32)], 0)


def unpack(packed, tail):
    ri = lax.broadcasted_iota(jnp.int32, (BLK, BLK), 0)
    ci = lax.broadcasted_iota(jnp.int32, (BLK, BLK), 1)
    blocks = {}
    for n, block in packed.items():
        turned = block.T
        if n < len(BELOW):
            i, j = BELOW[n]
            blocks[i, j], blocks[j, i] = block, turned
        else:
            m = 2 * (n - len(BELOW))
            diagonal = jnp.broadcast_to(tail[m // 2 : m // 2 + 1, :], (BLK, BLK))
            blocks[m, m] = jnp.where(ri >= ci, block, turned)
            blocks[m + 1, m + 1] = jnp.where(ri < ci, block, jnp.where(ri > ci, turned, diagonal))
    return blocks


def rows_of(ref, first=0):
    return {first + n: ref[BLK * n : BLK * n + BLK, :] for n in range(ref.shape[0] // BLK)}


def unpack_all(ref):
    return unpack(rows_of(ref), ref[BLK * PACKED :, :])


def unpack_first(ref):
    return unpack(rows_of(ref), None)


def unpack_second(ref):
    return unpack(rows_of(ref, FIRST), ref[BLK * (PACKED - FIRST) :, :])


def factor_block(block):
    ri = lax.broadcasted_iota(jnp.int32, (8, BLK), 0)
    ci = lax.broadcasted_iota(jnp.int32, (8, BLK), 1)
    count, wide = BLK // 8, 4
    left = [block[8 * t : 8 * t + 8, :] for t in range(count)]
    right = [jnp.where(ci == ri + 8 * t, 1.0, 0.0).astype(f32) for t in range(count)]
    upper, inverse = [], []
    here = [col(left[0], k) for k in range(8)]
    for s in range(count):
        end = (s // wide + 1) * wide
        ahead = {w: [col(left[w], 8 * s + k) for k in range(8)] for w in range(s + 1, min(end + 1, count))}
        following = [col(left[s + 1], 8 * s + 8 + k) for k in range(8)] if s + 1 < count else None
        a, t = left[s], right[s]
        pivots = None
        for k in range(8):
            pivot = row(here[k], k)
            inv = pl.reciprocal(pivot, approx=True)
            pivots = pivot if k == 0 else jnp.where(ri == k, pivot, pivots)
            mult = jnp.where(ri > k, here[k], 0.0) * inv
            rows = {m: row(here[m], k) for m in range(k + 1, 8)}
            row_a, row_t = row(a, k), row(t, k)
            for m in range(k + 1, 8):
                here[m] = here[m] - mult * rows[m]
            a = a - mult * row_a
            t = t - mult * row_t
            for w, cols in ahead.items():
                mult = cols[k] * inv
                if w == s + 1:
                    following = [f - mult * row(cols[k], m) for m, f in enumerate(following)]
                for m in range(k + 1, 8):
                    cols[m] = cols[m] - mult * rows[m]
                left[w] = left[w] - mult * row_a
                right[w] = right[w] - mult * row_t
        here = following
        scale = lax.rsqrt(pivots)
        upper.append(a * scale)
        inverse.append(t * scale)
        if s + 1 == end and end + 1 < count:
            ah, al = split(jnp.concatenate(upper[-wide:], 0))
            th, tl = split(jnp.concatenate(inverse[-wide:], 0))
            lhs = jnp.concatenate([ah, ah, al], 0)
            rhs_a = jnp.concatenate([ah, al, ah], 0)
            rhs_t = jnp.concatenate([th, tl, th], 0)
            outer = dot(lhs, jnp.concatenate([rhs_a, rhs_t], 1), TN)
            for q in range(end + 1, count):
                left[q] = left[q] - outer[8 * q : 8 * q + 8, :BLK]
                right[q] = right[q] - outer[8 * q : 8 * q + 8, BLK:]
    return jnp.concatenate(inverse, 0)


def factor(work, x, lower, inv, corner, gram=None, ready=None):
    ri = lax.broadcasted_iota(jnp.int32, (NS, BLK), 0)
    ci = lax.broadcasted_iota(jnp.int32, (NS, BLK), 1)

    def finish(k, inverse):
        here, then = at(BLK * k), at(BLK * jnp.minimum(k + 1, KS - 1))
        inv[k] = inverse
        pair = split(mm3(split(work[then, here]), split(inverse)))
        corner[...] = work[then, then] - mm3(pair, pair)

    def column(k):
        here = at(BLK * k)
        inverse = split(inv[k])
        panel = jnp.where(ri >= ci + BLK * k, mm3(split(work[:, here]), inverse), 0.0)
        lower[:, here] = panel
        return here, split(panel), mm3(split(x[:, here]), inverse)

    def update(k):
        here, pair, done = column(k)
        work[...] = work[...] - mm3(pair, pair)
        new = split(done)
        x[...] = x[...] - mm3(new, pair)
        x[:, here] = done
        if gram is not None:
            top = tuple(v[: gram.shape[0]] for v in new)
            gram[...] = gram[...] - mm3(top, top)

    def step(k, carry):
        inverse = factor_block(corner[...])
        update(k - 1)
        finish(k, inverse)
        return carry

    inverse = factor_block(work[0:BLK, 0:BLK])
    if ready is not None:
        ready()
    finish(0, inverse)
    lax.fori_loop(1, KS, step, 0)
    here, _, done = column(KS - 1)
    x[:, here] = done


def solve(x, lower, inv):
    for k in range(KS):
        o, e = BLK * k, BLK * (k + 1)
        done = mm3(split(x[:, o:e]), split(inv[k]))
        x[:, o:e] = done
        if k + 1 < KS:
            x[:, e:] = x[:, e:] - mm3(split(done), split(lower[e:, o:e]))


def ranks(values):
    out = []
    for a, va in enumerate(values):
        r = jnp.int32(0)
        for b, vb in enumerate(values):
            if a != b:
                r = r + (vb < va).astype(jnp.int32)
        out.append(r)
    return out


def sort_blocks(place, order):
    values = [place[0, a] for a in range(KB)]
    for a, r in enumerate(ranks(values)):
        order[r] = jnp.int32(a)


def at(start):
    return pl.ds(pl.multiple_of(start, BLK), BLK)


def corner_of(ref):
    return {
        (i, j): ref[BLK * i : BLK * i + BLK, BLK * j : BLK * j + BLK] for i in range(KS) for j in range(i + 1)
    }


def leaf_a(front, place_in, corner, w_out, lower, inv, a, next_block, ss, place, order, sems):
    copies = []
    for rows in (slice(0, BLK), slice(BLK, NS)):
        c = pltpu.make_async_copy(front.at[rows, 0:NS], a.at[rows, :], sems.at[len(copies)])
        c.start()
        copies.append(c)
    c = pltpu.make_async_copy(place_in, place, sems.at[len(copies)])
    c.start()
    c.wait()
    sort_blocks(place, order)
    for t in range(KS):
        c = pltpu.make_async_copy(
            front.at[at(NS + BLK * order[t]), 0:NS], w_out.at[BLK * t : BLK * t + BLK, :], sems.at[1 + len(copies)]
        )
        c.start()
        copies.append(c)
    for i in range(KS):
        for j in range(i + 1):
            c = pltpu.make_async_copy(
                front.at[at(NS + BLK * order[i]), at(NS + BLK * order[j])],
                ss.at[BLK * i : BLK * i + BLK, BLK * j : BLK * j + BLK],
                sems.at[1 + len(copies)],
            )
            c.start()
            copies.append(c)
    copies[0].wait()

    def ready():
        for c in copies[1:]:
            c.wait()

    factor(a, w_out, lower, inv, next_block, ss, ready)
    w = split(w_out[:, NS - BLK :])
    gram = mm3(w, w)
    blocks = {}
    for i in range(KS):
        for j in range(i + 1):
            rows, cols = slice(BLK * i, BLK * i + BLK), slice(BLK * j, BLK * j + BLK)
            blocks[i, j] = ss[rows, cols] - gram[rows, cols]

    def out(n, block):
        corner[BLK * n : BLK * n + BLK, :] = block

    corner[BLK * PACKED :, :] = pack(blocks, out)
    lane = lax.broadcasted_iota(jnp.int32, (1, BLK), 1)
    places = jnp.zeros((1, BLK), f32)
    for b in range(KB):
        places = jnp.where(lane == b, place[0, b].astype(f32), places)
    corner[PLACE_ROW : PLACE_ROW + 1, :] = places


def leaf_b(front, place_in, w, lower, inv, rs, rs_a, rs_b, rr_all, rr_a, rr_b, wr, f_rs, f_rr, place, order, sems):
    c = pltpu.make_async_copy(place_in, place, sems.at[KS * KB])
    c.start()
    c.wait()
    sort_blocks(place, order)
    copies = []
    for i in range(KS):
        c = pltpu.make_async_copy(
            front.at[at(NS + BLK * order[KS + i]), 0:NS], wr.at[BLK * i : BLK * i + BLK, :], sems.at[KS * KB + 1 + i]
        )
        c.start()
        copies.append(c)
    for i in range(KS):
        for j in range(KB):
            dst = f_rs if j < KS else f_rr
            c = pltpu.make_async_copy(
                front.at[at(NS + BLK * order[KS + i]), at(NS + BLK * order[j])],
                dst.at[BLK * i : BLK * i + BLK, BLK * (j % KS) : BLK * (j % KS) + BLK],
                sems.at[i * KB + j],
            )
            c.start()
            copies.append(c)
    for c in copies[:KS]:
        c.wait()
    solve(wr, lower, inv)
    ws, wr_pair = split(w[...]), split(wr[...])
    g_rs = mm3(wr_pair, ws)
    g_rr = mm3(wr_pair, wr_pair)
    for c in copies[KS:]:
        c.wait()
    rs[...] = f_rs[...] - g_rs
    rs_a[...] = rs[: NS // 2, :]
    rs_b[...] = rs[NS // 2 :, :]
    f_rr[...] = f_rr[...] - g_rr

    def out(n, block):
        rr_all[BLK * n : BLK * n + BLK, :] = block
        if n < FIRST:
            rr_a[BLK * n : BLK * n + BLK, :] = block
        else:
            rr_b[BLK * (n - FIRST) : BLK * (n - FIRST) + BLK, :] = block

    tail = pack(corner_of(f_rr), out)
    rr_all[BLK * PACKED :, :] = tail
    rr_b[BLK * (PACKED - FIRST) :, :] = tail


def merge_a(mine, other, rs, lower, inv, v, work, next_block):
    packed = {n: block + other[BLK * n : BLK * n + BLK, :] for n, block in rows_of(mine).items()}
    tail = mine[BLK * PACKED :, :] + other[BLK * PACKED :, :]
    for (i, j), block in unpack(packed, tail).items():
        work[BLK * i : BLK * i + BLK, BLK * j : BLK * j + BLK] = block
    v[...] = rs[...]
    factor(work, v, lower, inv, next_block)


def canonical(info, order):
    places = []
    for r in range(2):
        row_of = info.at[r : r + 1]
        sort_blocks(row_of, order)
        places += [row_of[0, order[KS + i]] for i in range(KS)]
    return [info[2, p - KS] for p in places]


def row_blocks(*parts):
    return [v.at[o : o + BLK, :] for v in parts for o in range(0, v.shape[0], BLK)]


def pair_update(rows, rr_low, spots, update, vs):
    where = ranks(spots)
    for e in range(KB):
        vs[at(BLK * where[e]), :] = rows[e][...]
    top, low = split(vs[0:NS, :]), split(vs[NS:, :])
    update[0:NS, 0:NS] = -mm3(top, top)
    update[NS:, 0:NS] = -mm3(low, top)
    update[NS:, NS:] = -mm3(low, low)
    for (i, j), block in unpack_all(rr_low).items():
        r, c = at(BLK * where[i]), at(BLK * where[j])
        update[r, c] = update[r, c] + block


def merge_b(lower, inv, rs_other, v):
    v[...] = rs_other[...]
    solve(v, lower, inv)


def assemble_mine(lower, v_mine, v_first, v_second, rr_low, info, panel, update, vs, order):
    rows = row_blocks(v_mine, v_first, v_second)
    pair_update(rows, rr_low, canonical(info, order), update, vs)
    panel[0:NS, :] = lower[...]
    for r in range(2):
        row_of = info.at[r : r + 1]
        sort_blocks(row_of, order)
        for i in range(KS):
            panel[at(BLK * row_of[0, order[KS + i]]), :] = rows[KS * r + i][...]


def assemble_other(v_mine, v_first, v_second, rr_low, info, update, vs, order):
    pair_update(row_blocks(v_mine, v_first, v_second), rr_low, canonical(info, order), update, vs)


def add_blocks(blocks, spots, ss=None, x=None, rr=None):
    for (i, j), block in blocks.items():
        si, sj = spots[i], spots[j]

        def add(part, cond, r, c):
            if part is not None:

                @pl.when(cond)
                def _():
                    part[at(BLK * r), at(BLK * c)] = part[at(BLK * r), at(BLK * c)] + block

        add(ss, (si < KS) & (sj < KS), si, sj)
        add(x, (si >= KS) & (sj < KS), si - KS, sj)
        add(rr, (si >= KS) & (sj >= KS), si - KS, sj - KS)


def join(up_a, up_b, low_a1, low_a2, low_b1, info_a, info_b, ss, x, rr, order):
    ss[...] = up_a[0:NS, 0:NS] + up_b[0:NS, 0:NS]
    rr[...] = jnp.zeros((NB, NB), f32)
    far = []
    for up, info in ((up_a, info_a), (up_b, info_b)):
        spots = canonical(info, order)
        far.append(spots[KS:])
        for spot, rank in zip(spots, ranks(spots)):
            order[rank] = spot
        for i in range(KS):
            r = at(BLK * (order[KS + i] - KS))
            rows = slice(NS + BLK * i, NS + BLK * i + BLK)
            x[r, :] = up[rows, 0:NS]
            for j in range(KS):
                rr[r, at(BLK * (order[KS + j] - KS))] = up[rows, NS + BLK * j : NS + BLK * j + BLK]
    add_blocks(unpack_first(low_a1), far[0], ss, x, rr)
    add_blocks(unpack_second(low_a2), far[0], ss, x, rr)
    add_blocks(unpack_first(low_b1), far[1], ss, x, rr)


def last(ss, x_in, rr, low, info, panel, update, work, x, lower, inv, next_block, buf, order, sems):
    fill_x = pltpu.make_async_copy(x_in, x, sems.at[3 + KB])
    fill = pltpu.make_async_copy(rr, buf, sems.at[0])
    fill_x.start()
    fill.start()
    work[...] = ss[...]
    far = canonical(info, order)[KS:]
    add_blocks(unpack_second(low), far, ss=work)

    def ready():
        fill_x.wait()
        add_blocks(unpack_second(low), far, x=x)

    factor(work, x, lower, inv, next_block, ready=ready)
    outs = [
        pltpu.make_async_copy(lower, panel.at[0:NS, :], sems.at[1]),
        pltpu.make_async_copy(x, panel.at[NS:, :], sems.at[2]),
    ]
    for c in outs:
        c.start()
    fill.wait()
    add_blocks(unpack_second(low), far, rr=buf)
    pair = split(x[...])
    wide = 2 * BLK
    for t in range(NB // wide):
        o, e = wide * t, wide * t + wide
        product = mm3(tuple(p[o:] for p in pair), tuple(p[o:e] for p in pair))
        buf[o:, o:e] = buf[o:, o:e] - product
        if e < NB:
            buf[o:e, e:] = buf[o:e, e:] - product[wide:].T
        c = pltpu.make_async_copy(buf.at[:, o:e], update.at[:, o:e], sems.at[3 + t])
        c.start()
        outs.append(c)
    for c in outs:
        c.wait()


def after(x, *earlier):
    return lax.optimization_barrier((x,) + earlier)[0]


def shards(leaf_front, place_pairs, place_quads):
    dma = pltpu.SemaphoreType.DMA
    half_cols = lax.axis_size("gx") // 2
    half_rows = lax.axis_size("gy") // 2

    def partner(x, axis):
        half = half_cols if axis == "gx" else half_rows
        return lax.ppermute(x, axis, [(i, (i + half) % (2 * half)) for i in range(2 * half)])

    def vmem(*shape):
        return pltpu.VMEM(shape, f32)

    order = pltpu.SMEM((KB,), jnp.int32)
    factor_scratch = [vmem(NS, NS), vmem(KS, BLK, BLK), vmem(BLK, BLK)]
    tri = sds(BLK * PACKED + 8, BLK)
    tri_a, tri_b = sds(BLK * FIRST, BLK), sds(BLK * (PACKED - FIRST) + 8, BLK)

    place = pltpu.SMEM((1, KB), jnp.int32)
    corner, w, lower, inv = call(
        leaf_a, (tri, sds(NS, NS), sds(NS, NS), sds(KS, BLK, BLK)), [HBM, HBM], [VMEM] * 4,
        [vmem(NS, NS), vmem(BLK, BLK), vmem(NS, NS), place, order, dma((3 + KS + KS * (KS + 1) // 2,))],
        (leaf_front, place_pairs), 48)
    corner_other = partner(corner, "gx")
    half = NS // 2
    rs, rs_a, rs_b, rr, rr_a, rr_b = call(
        leaf_b, (sds(NS, NS), sds(half, NS), sds(half, NS), tri, tri_a, tri_b), [HBM, HBM, VMEM, VMEM, VMEM], [VMEM] * 6,
        [vmem(NS, NS), vmem(NS, NS), vmem(NS, NS), place, order, dma((KS * KB + 1 + KS,))],
        (leaf_front, place_pairs, w, lower, inv), 48)
    rr_far = partner(rr, "gy")
    rs_first = partner(after(rs_a, corner_other), "gx")

    lower, inv, v_mine = call(
        merge_a, (sds(NS, NS), sds(KS, BLK, BLK), sds(NS, NS)), [VMEM] * 3, [VMEM] * 3,
        [vmem(NS, NS), vmem(BLK, BLK)], (corner, corner_other, rs), us=13)
    v_mine_far = partner(after(v_mine, rr_far), "gy")
    pairs_other = corner_other[PLACE_ROW : PLACE_ROW + 1, :KB].astype(jnp.int32)
    info = jnp.concatenate([place_pairs, pairs_other, place_quads], 0)
    info_other = partner(after(info, lower), "gy")
    rs_second = partner(after(rs_b, rs_first, lower), "gx")
    v_first = call(merge_b, sds(half, NS), [VMEM] * 3, VMEM, [], (lower, inv, rs_first))
    v_first_far = partner(v_first, "gy")
    rr_first = partner(after(rr_a, rs_second, v_mine_far, v_first_far), "gx")
    v_second = call(merge_b, sds(half, NS), [VMEM] * 3, VMEM, [], (lower, inv, rs_second))
    v_second_far = partner(v_second, "gy")
    scratch = [vmem(NB, NS), order]
    pair_panel, update = call(
        assemble_mine, (sds(NS + NB, NS), sds(NB, NB)), [VMEM] * 5 + [SMEM], [VMEM] * 2, scratch,
        (lower, v_mine, v_first, v_second, rr, info))
    rr_first, update, info_other = lax.optimization_barrier((rr_first, update, info_other))
    rr_second = partner(after(rr_b, rr_first), "gx")
    rr_first_far = partner(rr_first, "gy")
    update_far = call(
        assemble_other, sds(NB, NB), [VMEM] * 4 + [SMEM], VMEM, scratch,
        (v_mine_far, v_first_far, v_second_far, rr_far, info_other))
    rr_second_far = partner(after(rr_second, update_far), "gy")
    ss, x, rr = call(
        join, (sds(NS, NS), sds(NB, NS), sds(NB, NB)), [VMEM] * 5 + [SMEM] * 2, [VMEM] * 3, [order],
        (update, update_far, rr_first, rr_second, rr_first_far, info, info_other))
    quad_panel, quad_update = call(
        last, (sds(NS + NB, NS), sds(NB, NB)), [VMEM] * 4 + [SMEM], [HBM, HBM],
        [vmem(NS, NS), vmem(NB, NS)] + factor_scratch + [vmem(NB, NB), order, dma((4 + KB,))],
        (ss, x, rr, rr_second_far, info_other))
    return pair_panel, quad_panel, quad_update


def solution(mesh):
    spec = P("gx", "gy")
    return jax.shard_map(
        shards, mesh=mesh, in_specs=(spec, spec, spec), out_specs=(spec, spec, spec), check_vma=False
    )
```

```python
import jax
import jax.numpy as jnp
from jax import lax
from jax.experimental import pallas as pl
from jax.experimental.pallas import tpu as pltpu
from jax.sharding import PartitionSpec as P

f32 = jnp.float32
bf16 = jnp.bfloat16
NT = (((1,), (1,)), ((), ()))
TN = (((0,), (0,)), ((), ()))
BLK = 128
KB = 8
KS = 4
NS = KS * BLK
NB = KB * BLK
NJ = NS + NB
BELOW = [(a, b) for a in range(KS) for b in range(a)]
PACKED = len(BELOW) + KS // 2
FIRST = PACKED - 2
PLACE_ROW = BLK * PACKED + KS // 2
VMEM = pl.BlockSpec(memory_space=pltpu.VMEM)
SMEM = pl.BlockSpec(memory_space=pltpu.SMEM)
HBM = pl.BlockSpec(memory_space=pltpu.HBM)


def sds(*shape):
    return jax.ShapeDtypeStruct(shape, f32)


def call(body, out, ins, outs, scratch, args, vmem=24, us=0):
    return pl.pallas_call(
        body,
        out_shape=out,
        in_specs=ins,
        out_specs=outs,
        scratch_shapes=scratch,
        cost_estimate=pl.CostEstimate(flops=1000, bytes_accessed=1000 + int(us * 3.5e6), transcendentals=0),
        compiler_params=pltpu.CompilerParams(vmem_limit_bytes=vmem * 1024 * 1024),
    )(*args)


def split(x):
    hi = x.astype(bf16)
    return hi, (x - hi.astype(f32)).astype(bf16)


def dot(a, b, dims):
    return lax.dot_general(a, b, dims, preferred_element_type=f32)


def mm3(a, b):
    return dot(jnp.concatenate([a[0], a[0], a[1]], 1), jnp.concatenate([b[0], b[1], b[0]], 1), NT)


def row(x, k):
    return jnp.broadcast_to(x[k : k + 1, :], x.shape)


def col(x, j):
    return jnp.broadcast_to(x[:, j : j + 1], (8, BLK))


def pack(blocks, out):
    ri = lax.broadcasted_iota(jnp.int32, (BLK, BLK), 0)
    ci = lax.broadcasted_iota(jnp.int32, (BLK, BLK), 1)
    for n, key in enumerate(BELOW):
        out(n, blocks[key])
    diagonals = []
    for n in range(KS // 2):
        one, two = blocks[2 * n, 2 * n], blocks[2 * n + 1, 2 * n + 1]
        out(len(BELOW) + n, jnp.where(ri >= ci, one, two))
        diagonals.append(jnp.sum(jnp.where(ri == ci, two, 0.0), axis=0, keepdims=True))
    return jnp.concatenate(diagonals + [jnp.zeros((8 - len(diagonals), BLK), f32)], 0)


def unpack(packed, tail):
    ri = lax.broadcasted_iota(jnp.int32, (BLK, BLK), 0)
    ci = lax.broadcasted_iota(jnp.int32, (BLK, BLK), 1)
    blocks = {}
    for n, block in packed.items():
        turned = block.T
        if n < len(BELOW):
            i, j = BELOW[n]
            blocks[i, j], blocks[j, i] = block, turned
        else:
            m = 2 * (n - len(BELOW))
            diagonal = jnp.broadcast_to(tail[m // 2 : m // 2 + 1, :], (BLK, BLK))
            blocks[m, m] = jnp.where(ri >= ci, block, turned)
            blocks[m + 1, m + 1] = jnp.where(ri < ci, block, jnp.where(ri > ci, turned, diagonal))
    return blocks


def rows_of(ref, first=0):
    return {first + n: ref[BLK * n : BLK * n + BLK, :] for n in range(ref.shape[0] // BLK)}


def unpack_all(ref):
    return unpack(rows_of(ref), ref[BLK * PACKED :, :])


def unpack_first(ref):
    return unpack(rows_of(ref), None)


def unpack_second(ref):
    return unpack(rows_of(ref, FIRST), ref[BLK * (PACKED - FIRST) :, :])


def factor_block(block):
    ri = lax.broadcasted_iota(jnp.int32, (8, BLK), 0)
    ci = lax.broadcasted_iota(jnp.int32, (8, BLK), 1)
    count, wide = BLK // 8, 4
    left = [block[8 * t : 8 * t + 8, :] for t in range(count)]
    right = [jnp.where(ci == ri + 8 * t, 1.0, 0.0).astype(f32) for t in range(count)]
    upper, inverse = [], []
    here = [col(left[0], k) for k in range(8)]
    for s in range(count):
        end = (s // wide + 1) * wide
        ahead = {w: [col(left[w], 8 * s + k) for k in range(8)] for w in range(s + 1, min(end + 1, count))}
        following = [col(left[s + 1], 8 * s + 8 + k) for k in range(8)] if s + 1 < count else None
        a, t = left[s], right[s]
        pivots = None
        for k in range(8):
            pivot = row(here[k], k)
            inv = pl.reciprocal(pivot, approx=True)
            pivots = pivot if k == 0 else jnp.where(ri == k, pivot, pivots)
            mult = jnp.where(ri > k, here[k], 0.0) * inv
            rows = {m: row(here[m], k) for m in range(k + 1, 8)}
            row_a, row_t = row(a, k), row(t, k)
            for m in range(k + 1, 8):
                here[m] = here[m] - mult * rows[m]
            a = a - mult * row_a
            t = t - mult * row_t
            for w, cols in ahead.items():
                mult = cols[k] * inv
                if w == s + 1:
                    following = [f - mult * row(cols[k], m) for m, f in enumerate(following)]
                for m in range(k + 1, 8):
                    cols[m] = cols[m] - mult * rows[m]
                left[w] = left[w] - mult * row_a
                right[w] = right[w] - mult * row_t
        here = following
        scale = lax.rsqrt(pivots)
        upper.append(a * scale)
        inverse.append(t * scale)
        if s + 1 == end and end + 1 < count:
            ah, al = split(jnp.concatenate(upper[-wide:], 0))
            th, tl = split(jnp.concatenate(inverse[-wide:], 0))
            lhs = jnp.concatenate([ah, ah, al], 0)
            rhs_a = jnp.concatenate([ah, al, ah], 0)
            rhs_t = jnp.concatenate([th, tl, th], 0)
            outer = dot(lhs, jnp.concatenate([rhs_a, rhs_t], 1), TN)
            for q in range(end + 1, count):
                left[q] = left[q] - outer[8 * q : 8 * q + 8, :BLK]
                right[q] = right[q] - outer[8 * q : 8 * q + 8, BLK:]
    return jnp.concatenate(inverse, 0)


def factor(work, x, lower, inv, corner, gram=None, ready=None):
    ri = lax.broadcasted_iota(jnp.int32, (NS, BLK), 0)
    ci = lax.broadcasted_iota(jnp.int32, (NS, BLK), 1)

    def finish(k, inverse):
        here, then = at(BLK * k), at(BLK * jnp.minimum(k + 1, KS - 1))
        inv[k] = inverse
        pair = split(mm3(split(work[then, here]), split(inverse)))
        corner[...] = work[then, then] - mm3(pair, pair)

    def column(k):
        here = at(BLK * k)
        inverse = split(inv[k])
        panel = jnp.where(ri >= ci + BLK * k, mm3(split(work[:, here]), inverse), 0.0)
        lower[:, here] = panel
        return here, split(panel), mm3(split(x[:, here]), inverse)

    def update(k):
        here, pair, done = column(k)
        work[...] = work[...] - mm3(pair, pair)
        new = split(done)
        x[...] = x[...] - mm3(new, pair)
        x[:, here] = done
        if gram is not None:
            top = tuple(v[: gram.shape[0]] for v in new)
            gram[...] = gram[...] - mm3(top, top)

    def step(k, carry):
        inverse = factor_block(corner[...])
        update(k - 1)
        finish(k, inverse)
        return carry

    inverse = factor_block(work[0:BLK, 0:BLK])
    if ready is not None:
        ready()
    finish(0, inverse)
    lax.fori_loop(1, KS, step, 0)
    here, _, done = column(KS - 1)
    x[:, here] = done


def factor_unrolled(work, x, lower, inv, gram=None, ready=None):
    ri = lax.broadcasted_iota(jnp.int32, (BLK, BLK), 0)
    ci = lax.broadcasted_iota(jnp.int32, (BLK, BLK), 1)

    def update(k):
        o, e = BLK * k, BLK * k + BLK
        inverse = split(inv[k])
        panel = mm3(split(work[o:, o:e]), inverse)
        if k > 0:
            lower[0:o, o:e] = jnp.zeros((o, BLK), f32)
        lower[o:e, o:e] = jnp.where(ri >= ci, panel[:BLK], 0.0)
        done = mm3(split(x[:, o:e]), inverse)
        x[:, o:e] = done
        if k + 1 < KS:
            lower[e:, o:e] = panel[BLK:]
            pair = split(panel[BLK:])
            work[e:, e:] = work[e:, e:] - mm3(pair, pair)
            new = split(done)
            x[:, e:] = x[:, e:] - mm3(new, pair)
            if gram is not None:
                top = tuple(v[: gram.shape[0]] for v in new)
                gram[...] = gram[...] - mm3(top, top)

    block = work[0:BLK, 0:BLK]
    for k in range(KS):
        o, e = BLK * k, BLK * k + BLK
        inverse = factor_block(block)
        if k == 0 and ready is not None:
            ready()
        if k > 0:
            update(k - 1)
        inv[k] = inverse
        if k + 1 < KS:
            then = slice(e, e + BLK)
            pair = split(mm3(split(work[then, o:e]), split(inverse)))
            block = work[then, then] - mm3(pair, pair)
    update(KS - 1)


def solve(x, lower, inv):
    for k in range(KS):
        o, e = BLK * k, BLK * (k + 1)
        done = mm3(split(x[:, o:e]), split(inv[k]))
        x[:, o:e] = done
        if k + 1 < KS:
            x[:, e:] = x[:, e:] - mm3(split(done), split(lower[e:, o:e]))


def ranks(values):
    out = []
    for a, va in enumerate(values):
        r = jnp.int32(0)
        for b, vb in enumerate(values):
            if a != b:
                r = r + (vb < va).astype(jnp.int32)
        out.append(r)
    return out


def sort_blocks(place, order):
    values = [place[0, a] for a in range(KB)]
    for a, r in enumerate(ranks(values)):
        order[r] = jnp.int32(a)


def at(start):
    return pl.ds(pl.multiple_of(start, BLK), BLK)


def corner_of(ref):
    return {
        (i, j): ref[BLK * i : BLK * i + BLK, BLK * j : BLK * j + BLK] for i in range(KS) for j in range(i + 1)
    }


def leaf_a(front, place_in, corner, w_out, lower, inv, a, next_block, ss, place, order, sems):
    copies = []
    for rows in (slice(0, BLK), slice(BLK, NS)):
        c = pltpu.make_async_copy(front.at[rows, 0:NS], a.at[rows, :], sems.at[len(copies)])
        c.start()
        copies.append(c)
    c = pltpu.make_async_copy(place_in, place, sems.at[len(copies)])
    c.start()
    c.wait()
    sort_blocks(place, order)
    for t in range(KS):
        c = pltpu.make_async_copy(
            front.at[at(NS + BLK * order[t]), 0:NS], w_out.at[BLK * t : BLK * t + BLK, :], sems.at[1 + len(copies)]
        )
        c.start()
        copies.append(c)
    for i in range(KS):
        for j in range(i + 1):
            c = pltpu.make_async_copy(
                front.at[at(NS + BLK * order[i]), at(NS + BLK * order[j])],
                ss.at[BLK * i : BLK * i + BLK, BLK * j : BLK * j + BLK],
                sems.at[1 + len(copies)],
            )
            c.start()
            copies.append(c)
    copies[0].wait()

    def ready():
        for c in copies[1:]:
            c.wait()

    factor_unrolled(a, w_out, lower, inv, ss, ready)
    w = split(w_out[:, NS - BLK :])
    gram = mm3(w, w)
    blocks = {}
    for i in range(KS):
        for j in range(i + 1):
            rows, cols = slice(BLK * i, BLK * i + BLK), slice(BLK * j, BLK * j + BLK)
            blocks[i, j] = ss[rows, cols] - gram[rows, cols]

    def out(n, block):
        corner[BLK * n : BLK * n + BLK, :] = block

    corner[BLK * PACKED :, :] = pack(blocks, out)
    lane = lax.broadcasted_iota(jnp.int32, (1, BLK), 1)
    places = jnp.zeros((1, BLK), f32)
    for b in range(KB):
        places = jnp.where(lane == b, place[0, b].astype(f32), places)
    corner[PLACE_ROW : PLACE_ROW + 1, :] = places


def leaf_b(front, place_in, w, lower, inv, rs, rs_a, rs_b, rr_all, rr_a, rr_b, wr, f_rs, f_rr, place, order, sems):
    c = pltpu.make_async_copy(place_in, place, sems.at[KS * KB])
    c.start()
    c.wait()
    sort_blocks(place, order)
    copies = []
    for i in range(KS):
        c = pltpu.make_async_copy(
            front.at[at(NS + BLK * order[KS + i]), 0:NS], wr.at[BLK * i : BLK * i + BLK, :], sems.at[KS * KB + 1 + i]
        )
        c.start()
        copies.append(c)
    for i in range(KS):
        for j in range(KB):
            dst = f_rs if j < KS else f_rr
            c = pltpu.make_async_copy(
                front.at[at(NS + BLK * order[KS + i]), at(NS + BLK * order[j])],
                dst.at[BLK * i : BLK * i + BLK, BLK * (j % KS) : BLK * (j % KS) + BLK],
                sems.at[i * KB + j],
            )
            c.start()
            copies.append(c)
    for c in copies[:KS]:
        c.wait()
    solve(wr, lower, inv)
    ws, wr_pair = split(w[...]), split(wr[...])
    g_rs = mm3(wr_pair, ws)
    g_rr = mm3(wr_pair, wr_pair)
    for c in copies[KS:]:
        c.wait()
    rs[...] = f_rs[...] - g_rs
    rs_a[...] = rs[: NS // 2, :]
    rs_b[...] = rs[NS // 2 :, :]
    f_rr[...] = f_rr[...] - g_rr

    def out(n, block):
        rr_all[BLK * n : BLK * n + BLK, :] = block
        if n < FIRST:
            rr_a[BLK * n : BLK * n + BLK, :] = block
        else:
            rr_b[BLK * (n - FIRST) : BLK * (n - FIRST) + BLK, :] = block

    tail = pack(corner_of(f_rr), out)
    rr_all[BLK * PACKED :, :] = tail
    rr_b[BLK * (PACKED - FIRST) :, :] = tail


def merge_a(mine, other, rs, lower, inv, v, work, next_block):
    packed = {n: block + other[BLK * n : BLK * n + BLK, :] for n, block in rows_of(mine).items()}
    tail = mine[BLK * PACKED :, :] + other[BLK * PACKED :, :]
    for (i, j), block in unpack(packed, tail).items():
        work[BLK * i : BLK * i + BLK, BLK * j : BLK * j + BLK] = block
    v[...] = rs[...]
    factor(work, v, lower, inv, next_block)


def canonical(info, order):
    places = []
    for r in range(2):
        row_of = info.at[r : r + 1]
        sort_blocks(row_of, order)
        places += [row_of[0, order[KS + i]] for i in range(KS)]
    return [info[2, p - KS] for p in places]


def row_blocks(*parts):
    return [v.at[o : o + BLK, :] for v in parts for o in range(0, v.shape[0], BLK)]


def pair_update(rows, rr_low, spots, update, vs):
    where = ranks(spots)
    for e in range(KB):
        vs[at(BLK * where[e]), :] = rows[e][...]
    top, low = split(vs[0:NS, :]), split(vs[NS:, :])
    update[0:NS, 0:NS] = -mm3(top, top)
    update[NS:, 0:NS] = -mm3(low, top)
    update[NS:, NS:] = -mm3(low, low)
    for (i, j), block in unpack_all(rr_low).items():
        r, c = at(BLK * where[i]), at(BLK * where[j])
        update[r, c] = update[r, c] + block


def merge_b(lower, inv, rs_other, v):
    v[...] = rs_other[...]
    solve(v, lower, inv)


def assemble_mine(lower, v_mine, v_first, v_second, rr_low, info, panel, update, vs, order):
    rows = row_blocks(v_mine, v_first, v_second)
    pair_update(rows, rr_low, canonical(info, order), update, vs)
    panel[0:NS, :] = lower[...]
    for r in range(2):
        row_of = info.at[r : r + 1]
        sort_blocks(row_of, order)
        for i in range(KS):
            panel[at(BLK * row_of[0, order[KS + i]]), :] = rows[KS * r + i][...]


def assemble_other(v_mine, v_first, v_second, rr_low, info, update, vs, order):
    pair_update(row_blocks(v_mine, v_first, v_second), rr_low, canonical(info, order), update, vs)


def add_blocks(blocks, spots, ss=None, x=None, rr=None):
    for (i, j), block in blocks.items():
        si, sj = spots[i], spots[j]

        def add(part, cond, r, c):
            if part is not None:

                @pl.when(cond)
                def _():
                    part[at(BLK * r), at(BLK * c)] = part[at(BLK * r), at(BLK * c)] + block

        add(ss, (si < KS) & (sj < KS), si, sj)
        add(x, (si >= KS) & (sj < KS), si - KS, sj)
        add(rr, (si >= KS) & (sj >= KS), si - KS, sj - KS)


def join(up_a, up_b, low_a1, low_a2, low_b1, info_a, info_b, ss, x, rr, order):
    ss[...] = up_a[0:NS, 0:NS] + up_b[0:NS, 0:NS]
    rr[...] = jnp.zeros((NB, NB), f32)
    far = []
    for up, info in ((up_a, info_a), (up_b, info_b)):
        spots = canonical(info, order)
        far.append(spots[KS:])
        for spot, rank in zip(spots, ranks(spots)):
            order[rank] = spot
        for i in range(KS):
            r = at(BLK * (order[KS + i] - KS))
            rows = slice(NS + BLK * i, NS + BLK * i + BLK)
            x[r, :] = up[rows, 0:NS]
            for j in range(KS):
                rr[r, at(BLK * (order[KS + j] - KS))] = up[rows, NS + BLK * j : NS + BLK * j + BLK]
    add_blocks(unpack_first(low_a1), far[0], ss, x, rr)
    add_blocks(unpack_second(low_a2), far[0], ss, x, rr)
    add_blocks(unpack_first(low_b1), far[1], ss, x, rr)


def last(ss, x_in, rr, low, info, panel, update, work, x, lower, inv, next_block, buf, order, sems):
    fill_x = pltpu.make_async_copy(x_in, x, sems.at[3 + KB])
    fill = pltpu.make_async_copy(rr, buf, sems.at[0])
    fill_x.start()
    fill.start()
    work[...] = ss[...]
    far = canonical(info, order)[KS:]
    add_blocks(unpack_second(low), far, ss=work)

    def ready():
        fill_x.wait()
        add_blocks(unpack_second(low), far, x=x)

    factor(work, x, lower, inv, next_block, ready=ready)
    outs = [
        pltpu.make_async_copy(lower, panel.at[0:NS, :], sems.at[1]),
        pltpu.make_async_copy(x, panel.at[NS:, :], sems.at[2]),
    ]
    for c in outs:
        c.start()
    fill.wait()
    add_blocks(unpack_second(low), far, rr=buf)
    pair = split(x[...])
    wide = 2 * BLK
    for t in range(NB // wide):
        o, e = wide * t, wide * t + wide
        product = mm3(tuple(p[o:] for p in pair), tuple(p[o:e] for p in pair))
        buf[o:, o:e] = buf[o:, o:e] - product
        if e < NB:
            buf[o:e, e:] = buf[o:e, e:] - product[wide:].T
        c = pltpu.make_async_copy(buf.at[:, o:e], update.at[:, o:e], sems.at[3 + t])
        c.start()
        outs.append(c)
    for c in outs:
        c.wait()


def after(x, *earlier):
    return lax.optimization_barrier((x,) + earlier)[0]


def shards(leaf_front, place_pairs, place_quads):
    dma = pltpu.SemaphoreType.DMA
    half_cols = lax.axis_size("gx") // 2
    half_rows = lax.axis_size("gy") // 2

    def partner(x, axis):
        half = half_cols if axis == "gx" else half_rows
        return lax.ppermute(x, axis, [(i, (i + half) % (2 * half)) for i in range(2 * half)])

    def vmem(*shape):
        return pltpu.VMEM(shape, f32)

    order = pltpu.SMEM((KB,), jnp.int32)
    factor_scratch = [vmem(NS, NS), vmem(KS, BLK, BLK), vmem(BLK, BLK)]
    tri = sds(BLK * PACKED + 8, BLK)
    tri_a, tri_b = sds(BLK * FIRST, BLK), sds(BLK * (PACKED - FIRST) + 8, BLK)

    place = pltpu.SMEM((1, KB), jnp.int32)
    corner, w, lower, inv = call(
        leaf_a, (tri, sds(NS, NS), sds(NS, NS), sds(KS, BLK, BLK)), [HBM, HBM], [VMEM] * 4,
        [vmem(NS, NS), vmem(BLK, BLK), vmem(NS, NS), place, order, dma((3 + KS + KS * (KS + 1) // 2,))],
        (leaf_front, place_pairs), 48)
    corner_other = partner(corner, "gx")
    half = NS // 2
    rs, rs_a, rs_b, rr, rr_a, rr_b = call(
        leaf_b, (sds(NS, NS), sds(half, NS), sds(half, NS), tri, tri_a, tri_b), [HBM, HBM, VMEM, VMEM, VMEM], [VMEM] * 6,
        [vmem(NS, NS), vmem(NS, NS), vmem(NS, NS), place, order, dma((KS * KB + 1 + KS,))],
        (leaf_front, place_pairs, w, lower, inv), 48)
    rr_far = partner(rr, "gy")
    rs_first = partner(after(rs_a, corner_other), "gx")

    lower, inv, v_mine = call(
        merge_a, (sds(NS, NS), sds(KS, BLK, BLK), sds(NS, NS)), [VMEM] * 3, [VMEM] * 3,
        [vmem(NS, NS), vmem(BLK, BLK)], (corner, corner_other, rs), us=13)
    v_mine_far = partner(after(v_mine, rr_far), "gy")
    pairs_other = corner_other[PLACE_ROW : PLACE_ROW + 1, :KB].astype(jnp.int32)
    info = jnp.concatenate([place_pairs, pairs_other, place_quads], 0)
    info_other = partner(after(info, lower), "gy")
    rs_second = partner(after(rs_b, rs_first, lower), "gx")
    v_first = call(merge_b, sds(half, NS), [VMEM] * 3, VMEM, [], (lower, inv, rs_first))
    v_first_far = partner(v_first, "gy")
    rr_first = partner(after(rr_a, rs_second, v_mine_far, v_first_far), "gx")
    v_second = call(merge_b, sds(half, NS), [VMEM] * 3, VMEM, [], (lower, inv, rs_second))
    v_second_far = partner(v_second, "gy")
    scratch = [vmem(NB, NS), order]
    pair_panel, update = call(
        assemble_mine, (sds(NS + NB, NS), sds(NB, NB)), [VMEM] * 5 + [SMEM], [VMEM] * 2, scratch,
        (lower, v_mine, v_first, v_second, rr, info))
    rr_first, update, info_other = lax.optimization_barrier((rr_first, update, info_other))
    rr_second = partner(after(rr_b, rr_first), "gx")
    rr_first_far = partner(rr_first, "gy")
    update_far = call(
        assemble_other, sds(NB, NB), [VMEM] * 4 + [SMEM], VMEM, scratch,
        (v_mine_far, v_first_far, v_second_far, rr_far, info_other))
    rr_second_far = partner(after(rr_second, update_far), "gy")
    ss, x, rr = call(
        join, (sds(NS, NS), sds(NB, NS), sds(NB, NB)), [VMEM] * 5 + [SMEM] * 2, [VMEM] * 3, [order],
        (update, update_far, rr_first, rr_second, rr_first_far, info, info_other))
    quad_panel, quad_update = call(
        last, (sds(NS + NB, NS), sds(NB, NB)), [VMEM] * 4 + [SMEM], [HBM, HBM],
        [vmem(NS, NS), vmem(NB, NS)] + factor_scratch + [vmem(NB, NB), order, dma((4 + KB,))],
        (ss, x, rr, rr_second_far, info_other))
    return pair_panel, quad_panel, quad_update


def solution(mesh):
    spec = P("gx", "gy")
    return jax.shard_map(
        shards, mesh=mesh, in_specs=(spec, spec, spec), out_specs=(spec, spec, spec), check_vma=False
    )
```
